256 devices in a mesh: row: 8 (over z_hi, core), col: 4 (over y), depth: 8 (over z_lo, x).
Axes of the slice: x: 4, y: 4, z: 8 (z_hi: 4, z_lo: 2; z = z_hi * 2 + z_lo), core: 2. Of those that a mesh axis runs over, the one named last changes fastest.
Arguments:
- tokens: bfloat16 [6144, 2560], P(('col', 'depth'), 'row'), may hold values from -6 to 6
- up_weight: bfloat16 [2560, 10240], P('col', 'row'), may hold values from -0.125 to 0.125
- up_bias: float32 [10240], P('row'), may hold values from -3 to 3
- down_weight: bfloat16 [10240, 2560], P('col', 'row'), may hold values from -0.0625 to 0.0625
- down_bias: float32 [2560], P('row'), may hold values from -3 to 3
- out_grad: bfloat16 [6144, 2560], P(('col', 'depth'), 'row'), may hold values from -6 to 6
Outputs:
- layer_out: bfloat16 [6144, 2560], P(('col', 'depth'), 'row')
- grad_in: bfloat16 [6144, 2560], P(('col', 'depth'), 'row')
- grad_up: bfloat16 [2560, 10240], P('col', 'row')
- grad_up_bias: bfloat16 [10240], P('row')
- grad_down: bfloat16 [10240, 2560], P('col', 'row')
- grad_down_bias: bfloat16 [2560], P('row')
The draws below stay inside these ranges and needn't reach their ends.
All inputs are finite; a program needn't handle non-finite values.
Results may differ from the reference program's by a relative error of at most 0.029.
Values may be sent and summed in bfloat16 or wider, within the bound.
A program may use at most 128 MiB of HBM per device.

```python
import math
import jax
import jax.numpy as jnp
from jax import lax

D = 2560
FF = 10240
TOK_DEV = 192
TOKENS = 6144
N_ROW = 8
N_COL = 4
N_DEPTH = 8


def block_scale(key, extent, split, low, largest):
    def one(dim, blocks):
        steps = jax.random.uniform(jax.random.fold_in(jax.random.fold_in(key, 6), dim), (blocks,), jnp.float32, low / len(split), largest / len(split))
        return jnp.repeat(jnp.exp(steps), extent[dim] // blocks).reshape((-1,) + (1,) * (len(extent) - dim - 1))

    factor_of = one(*split[0])
    for cut in split[1:]:
        factor_of = factor_of * one(*cut)
    return factor_of


def centred(key, extent, deviation, most, split=(), kind=jnp.bfloat16):
    entries = deviation * jax.random.normal(key, extent, jnp.float32)
    if split:
        entries = entries * block_scale(key, extent, split, -0.22, 0.18)
    return jnp.clip(entries, -most, most).astype(kind)


def setup_inputs(seed: int = 0) -> dict:
    arg_keys = jax.random.split(jax.random.key(seed), 7)
    tokens = centred(arg_keys[0], (TOKENS, D), 1.0, 6.0, ((0, 32), (1, 8)))
    up_weight = centred(arg_keys[1], (D, FF), D ** -0.5, 0.125, ((0, 4), (1, 8)))
    up_bias = centred(arg_keys[2], (FF,), 0.5, 3.0, ((0, 8),), jnp.float32)
    down_weight = centred(arg_keys[3], (FF, D), FF ** -0.5, 0.0625, ((0, 4), (1, 8)))
    down_bias = centred(arg_keys[4], (D,), 0.5, 3.0, ((0, 8),), jnp.float32)
    out_grad = centred(arg_keys[5], (TOKENS, D), 1.0, 6.0, ((0, 32), (1, 8)))
    return dict(tokens=tokens, up_weight=up_weight, up_bias=up_bias, down_weight=down_weight, down_bias=down_bias, out_grad=out_grad)


GELU_C = math.sqrt(2.0 / math.pi)

def gelu_parts(hidden_pre):
    tanh_arg = GELU_C * (hidden_pre + 0.044715 * hidden_pre * hidden_pre * hidden_pre)
    tanh_val = jnp.tanh(tanh_arg)
    gelu_value = 0.5 * hidden_pre * (1.0 + tanh_val)
    gelu_slope = 0.5 * (1.0 + tanh_val) + 0.5 * hidden_pre * (1.0 - tanh_val * tanh_val) * GELU_C * (1.0 + 3.0 * 0.044715 * hidden_pre * hidden_pre)
    return (gelu_value, gelu_slope)

def block_contract(left_side, weight):
    inner = left_side.shape[1]
    block = inner // N_ROW

    def add_block(carry, index):
        start = (index * block).astype(jnp.int32)
        left_piece = lax.dynamic_slice_in_dim(left_side, start, block, 1)
        weight_piece = lax.dynamic_slice_in_dim(weight, start, block, 1)
        term = jnp.dot(left_piece, weight_piece.T, preferred_element_type=jnp.float32)
        term = lax.optimization_barrier(term.astype(jnp.bfloat16)).astype(jnp.float32)
        return (carry + term, None)
    start_sum = jnp.zeros((left_side.shape[0], weight.shape[0]), jnp.float32)
    total, _ = lax.scan(add_block, start_sum, jnp.arange(N_ROW, dtype=jnp.int32))
    return total

def depth_sums(left_side, right_side, grad_scale):
    width_left = left_side.shape[1]
    width_right = right_side.shape[1]
    left_groups = left_side.reshape(N_COL, N_DEPTH, TOK_DEV, width_left)
    right_groups = right_side.reshape(N_COL, N_DEPTH, TOK_DEV, width_right)

    def add_group(carry, group):
        left_piece = lax.dynamic_index_in_dim(left_groups, group, 1, keepdims=False).reshape(N_COL * TOK_DEV, width_left)
        right_piece = lax.dynamic_index_in_dim(right_groups, group, 1, keepdims=False).reshape(N_COL * TOK_DEV, width_right)
        matrix_term = jnp.dot(left_piece.T, right_piece, preferred_element_type=jnp.float32) * grad_scale
        column_term = lax.optimization_barrier(jnp.sum(right_piece.astype(jnp.float32), axis=0)) * grad_scale
        matrix_term = lax.optimization_barrier(matrix_term.astype(jnp.bfloat16)).astype(jnp.float32)
        column_term = lax.optimization_barrier(column_term.astype(jnp.bfloat16)).astype(jnp.float32)
        return ((carry[0] + matrix_term, carry[1] + column_term), None)
    start_sums = (jnp.zeros((width_left, width_right), jnp.float32), jnp.zeros((width_right,), jnp.float32))
    (matrix_sum, column_sum), _ = lax.scan(add_group, start_sums, jnp.arange(N_DEPTH, dtype=jnp.int32))
    return (matrix_sum.astype(jnp.bfloat16), column_sum.astype(jnp.bfloat16))

def reference(tokens, up_weight, up_bias, down_weight, down_bias, out_grad):
    hidden_pre = jnp.dot(tokens, up_weight, preferred_element_type=jnp.float32) + up_bias
    gelu_value, gelu_slope = gelu_parts(hidden_pre)
    activ = gelu_value.astype(jnp.bfloat16)
    layer_out = (jnp.dot(activ, down_weight, preferred_element_type=jnp.float32) + down_bias).astype(jnp.bfloat16)
    d_act = block_contract(out_grad, down_weight)
    d_hidden = (d_act * gelu_slope).astype(jnp.bfloat16)
    grad_in = block_contract(d_hidden, up_weight).astype(jnp.bfloat16)
    grad_scale = 1.0 / math.sqrt(TOKENS)
    grad_up, grad_up_bias = depth_sums(tokens, d_hidden, grad_scale)
    grad_down, grad_down_bias = depth_sums(activ, out_grad, grad_scale)
    return (layer_out, grad_in, grad_up, grad_up_bias, grad_down, grad_down_bias)
```

```python
import math

import jax
import jax.numpy as jnp
from jax import lax
from jax.experimental import pallas as pl
from jax.experimental.pallas import tpu as pltpu
from jax.sharding import PartitionSpec as P

GELU_C = math.sqrt(2.0 / math.pi)
MESH = pl.DeviceIdType.MESH
F32 = jnp.float32
BF16 = jnp.bfloat16
N_SEMS = 320


def gelu_parts(v):
    t = jnp.tanh(GELU_C * (v + 0.044715 * v * v * v))
    value = 0.5 * v * (1.0 + t)
    slope = 0.5 * (1.0 + t) + 0.5 * v * (1.0 - t * t) * GELU_C * (1.0 + 3.0 * 0.044715 * v * v)
    return value, slope


def nn(a, b):
    return lax.dot_general(a, b, (((1,), (0,)), ((), ())), preferred_element_type=F32)


def nt(a, b):
    return lax.dot_general(a, b, (((1,), (1,)), ((), ())), preferred_element_type=F32)


def rows(start, size, tile=16):
    return pl.ds(pl.multiple_of(start, tile), size)


def kernel(
    scale,
    tok, wu_in, bu_in, wd_in, bd_in, grad,
    o_out, gi_out, gu_out, gd_out, bu_out, bd_out,
    xr, piece, wdo, wdr, wdq, bb, bbr,
    full, wts, full_t,
    hps, hpr, hpo, slope, act, act_t, dps, dpr, dhid,
    part, ra, rb, xsum, zr, osend, orecv,
    gpart, ga, gb, gsum, gz, gfin, rd, rdo, rds,
    bt, br, yb, pb,
    sems,
):
    row, y, dep = lax.axis_index("row"), lax.axis_index("col"), lax.axis_index("depth")
    h, k = row // 2, lax.rem(row, 2)
    zl, x = dep // 4, lax.rem(dep, 4)
    dd = x * 2 + zl
    hh = h // 2
    hi = lax.rem(h, 2)

    def at(h_, k_, y_):
        return (h_ * 2 + k_, y_, dep)

    def dep_at(a, b):
        return (row, y, lax.rem(zl + b, 2) * 4 + lax.rem(x + a, 4))

    def y_at(a):
        return (row, lax.rem(y + a, 4), dep)

    partner = (h * 2 + 1 - k, y, dep)
    zpeer = dep_at(0, 1)

    bar = pltpu.get_barrier_semaphore()
    fixed = [partner] + [y_at(a) for a in (1, 2, 3)]
    fixed += [dep_at(a, b) for a in range(4) for b in range(2) if (a, b) != (0, 0)]
    for target in fixed:
        pl.semaphore_signal(bar, inc=1, device_id=target, device_id_type=MESH)
    count = len(fixed)

    def greet(h_, k_, y_):
        other = jnp.logical_not((h_ == h) & (k_ == k) & (y_ == y))

        @pl.when(other)
        def _():
            pl.semaphore_signal(bar, inc=1, device_id=at(h_, k_, y_), device_id_type=MESH)

        return other.astype(jnp.int32)

    for a in range(4):
        count = count + greet(a, hh, y)
    for a in range(2):
        for b in range(2):
            count = count + greet(2 * k + a, b, y)
    for j in range(2):
        count = count + greet(h, y // 2, 2 * k + j)
        count = count + greet(y, hh, 2 * k + j)
        count = count + greet(2 * k + j, y // 2, h)
    pl.semaphore_wait(bar, count)

    used = [0]
    sent = []

    def new(n=1):
        first = used[0]
        used[0] += n
        return first

    def send(src, dst, rsem, target):
        copy = pltpu.make_async_remote_copy(
            src_ref=src, dst_ref=dst, send_sem=sems.at[new()], recv_sem=sems.at[rsem],
            device_id=target, device_id_type=MESH,
        )
        copy.start()
        sent.append((copy, None))

    def send_maybe(src, dst, rsem, h_, k_, y_):
        mine = (h_ == h) & (k_ == k) & (y_ == y)
        copy = pltpu.make_async_remote_copy(
            src_ref=src, dst_ref=dst, send_sem=sems.at[new()], recv_sem=sems.at[rsem],
            device_id=at(h_, k_, y_), device_id_type=MESH,
        )

        @pl.when(jnp.logical_not(mine))
        def _():
            copy.start()

        @pl.when(mine)
        def _():
            pltpu.make_async_copy(src, dst, sems.at[rsem]).start()

        sent.append((copy, jnp.logical_not(mine)))

    def got(dst, rsem):
        pltpu.make_async_copy(dst, dst, sems.at[rsem]).wait()

    def ring(axis):
        if axis == "y":
            return y, y_at(1), y_at(3)
        return x, dep_at(1, 0), dep_at(3, 0)

    class Gather:
        def __init__(self, buf, size, axis):
            self.p, self.right, self.left = ring(axis)
            self.view = lambda i, q: buf.at[i, rows(lax.rem(q, 4) * size, size)]
            self.s_right = new(2)
            self.s_left = new(2)
            self.s_fwd = new(2)

        def first(self, i):
            mine = self.view(i, self.p)
            pair = [(self.s_right + i, self.right), (self.s_left + i, self.left)]
            for sem, target in pair if i == 0 else pair[::-1]:
                send(mine, mine, sem, target)

        def forward(self, i):
            if i == 0:
                block = self.view(0, self.p + 3)
                got(block, self.s_right)
                send(block, block, self.s_fwd, self.right)
            else:
                block = self.view(1, self.p + 1)
                got(block, self.s_left + 1)
                send(block, block, self.s_fwd + 1, self.left)

        def finish(self):
            got(self.view(1, self.p + 3), self.s_right + 1)
            got(self.view(0, self.p + 1), self.s_left)
            got(self.view(0, self.p + 2), self.s_fwd)
            got(self.view(1, self.p + 2), self.s_fwd + 1)

    class Reduce:
        def __init__(self, buf, first, second, size, axis):
            self.p, self.right, self.left = ring(axis)
            self.view = lambda i, q: buf.at[i, rows(lax.rem(q, 4) * size, size)]
            self.first, self.second = first, second
            self.s1, self.s2 = new(2), new(4)

        def far(self):
            send(self.view(0, self.p + 2), self.first.at[0], self.s1, self.right)
            send(self.view(1, self.p + 2), self.first.at[1], self.s1 + 1, self.left)

        def near(self):
            send(self.view(1, self.p + 1), self.second.at[0, 1], self.s2 + 1, self.right)
            send(self.view(0, self.p + 3), self.second.at[1, 0], self.s2 + 2, self.left)

        def middle(self):
            for i, q, target in ((0, self.p + 1, self.right), (1, self.p + 3, self.left)):
                got(self.first.at[i], self.s1 + i)
                block = self.view(i, q)
                block[...] = (block[...].astype(F32) + self.first[i].astype(F32)).astype(BF16)
                send(block, self.second.at[i, i], self.s2 + 3 * i, target)

        def total(self, i):
            got(self.second.at[0, i], self.s2 + i)
            got(self.second.at[1, i], self.s2 + 2 + i)
            return (
                self.view(i, self.p)[...].astype(F32)
                + self.second[0, i].astype(F32)
                + self.second[1, i].astype(F32)
            )

    def pair_lanes(own, other):
        first = jnp.where(k == 0, own, other).astype(F32)
        second = jnp.where(k == 0, other, own).astype(F32)
        return jnp.concatenate([first, second], axis=1).astype(BF16)

    def split_lanes(both):
        low, high = both[:, :320], both[:, 320:]
        return jnp.where(k == 0, low, high), jnp.where(k == 0, high, low)

    s_x = new(2)
    for n, src in enumerate((tok, grad)):
        send(src.at[rows((1 - k) * 96, 96)], xr.at[n], s_x + n, partner)
    s_wu = new(2)
    for j in range(2):
        send_maybe(
            wu_in.at[rows(dd * 80, 80), pl.ds(j * 640, 640)],
            wts.at[0, lax.rem(y, 2), rows(dd * 80, 80)],
            s_wu + lax.rem(y, 2), h, y // 2, 2 * k + j,
        )
    s_wd = new(1)
    send(wd_in.at[pl.ds(2 * (1 - k), 2), rows(dd * 80, 80)], wdr, s_wd, partner)
    s_wo = new(1)
    own_wd = pltpu.make_async_copy(wd_in.at[pl.ds(2 * k, 2), rows(dd * 80, 80)], wdo, sems.at[s_wo])
    own_wd.start()
    bb[...] = jnp.broadcast_to(bu_in[...], bb.shape)
    s_bb = new(1)
    send(bb, bbr, s_bb, partner)

    s_piece = [new(4), new(4)]

    def send_piece(n, src):
        got(xr.at[n], s_x + n)
        piece[n] = pair_lanes(src[rows(k * 96, 96), :], xr[n])
        for a in range(4):
            hz = lax.rem(h + a, 4)
            send_maybe(
                piece.at[n],
                full.at[n, hi, rows(y * 192 + k * 96, 96)],
                s_piece[n] + hi * 2 + k, hz, hh, y,
            )

    def got_pieces(n, i):
        for kk in range(2):
            got(full.at[n, i, rows(y * 192 + kk * 96, 96)], s_piece[n] + i * 2 + kk)

    send_piece(0, tok)

    own_wd.wait()
    got(wdr, s_wd)
    s_wd2 = new(2)
    for j in range(2):
        wdq[j] = pair_lanes(wdo[j], wdr[j])
    for j in range(2):
        send_maybe(
            wdq.at[j], wts.at[1, hi, rows(dd * 80, 80)], s_wd2 + hi, y, hh, 2 * k + j,
        )
    send_piece(1, grad)

    s_zl = new(2)

    def over_zl(n):
        mine = wts.at[n, :, rows(dd * 80, 80)]
        for i in range(2):
            got(wts.at[n, i, rows(dd * 80, 80)], (s_wu if n == 0 else s_wd2) + i)
        send(mine, mine, s_zl + n, zpeer)

    def got_zl(n):
        got(wts.at[n, :, rows((x * 2 + 1 - zl) * 80, 80)], s_zl + n)

    wag = [Gather(wts.at[n], 160, "x") for n in range(2)]
    tag = [Gather(full.at[n], 192, "y") for n in range(2)]

    over_zl(0)
    for i in range(2):
        got_pieces(0, i)
        tag[0].first(i)
    got_zl(0)
    for i in range(2):
        wag[0].first(i)
    over_zl(1)
    for i in range(2):
        tag[0].forward(i)
    for i in range(2):
        wag[0].forward(i)
    got_zl(1)
    for i in range(2):
        wag[1].first(i)
    for i in range(2):
        got_pieces(1, i)
        tag[1].first(i)

    half = 384
    own_rows = rows(k * half, half)
    other_rows = rows((1 - k) * half, half)
    tag[0].finish()
    for i in range(2):
        full_t[i] = full[0, i].T
    wag[0].finish()
    for i in range(2):
        tag[1].forward(i)
    for i in range(2):
        wag[1].forward(i)
    s_hp, s_act, s_dp, s_dh = new(1), new(1), new(1), new(1)
    hps[...] = nn(full[0, 0, other_rows], wts[0, 0]) + nn(full[0, 1, other_rows], wts[0, 1])
    send(hps, hpr, s_hp, partner)
    hpo[...] = nn(full[0, 0, own_rows], wts[0, 0]) + nn(full[0, 1, own_rows], wts[0, 1])
    got(bbr, s_bb)
    low = jnp.where(k == y // 2, bb[0:1], bbr[0:1])
    bias = jnp.where(lax.rem(y, 2) == 0, low[:, :640], low[:, 640:])
    got(hpr, s_hp)
    value, slope_now = gelu_parts(hpo[...] + hpr[...] + bias)
    slope[...] = slope_now
    act[own_rows] = value.astype(BF16)
    send(act.at[own_rows], act.at[own_rows], s_act, partner)

    tag[1].finish()
    wag[1].finish()
    dps[...] = nt(full[1, 0, other_rows], wts[1, 0]) + nt(full[1, 1, other_rows], wts[1, 1])
    send(dps, dpr, s_dp, partner)
    got(act.at[other_rows], s_act)
    act_t[...] = act[...].T

    ored = [Reduce(part.at[n], ra.at[n], rb.at[n], 192, "y") for n in range(2)]
    gred = [Reduce(gpart.at[n], ga.at[n], gb.at[n], 160, "x") for n in range(2)]

    def out_block(n, q):
        block = rows(lax.rem(q, 4) * 192, 192)
        for i in range(2):
            if n == 0:
                part[0, i, block] = nn(act[block], wts[1, i]).astype(BF16)
            else:
                part[1, i, block] = nt(dhid[block], wts[0, i]).astype(BF16)

    def grad_block(n, q):
        block = rows(lax.rem(q, 4) * 160, 160)
        for i in range(2):
            if n == 0:
                term = nn(full_t[i, block], dhid[...])
            else:
                term = nn(act_t[block], full[1, i])
            gpart[n, i, block] = (term * scale).astype(BF16)

    out_block(0, y + 2)
    ored[0].far()
    grad_block(1, x + 2)
    gred[1].far()
    out_block(0, y + 1)
    out_block(0, y + 3)
    ored[0].near()
    grad_block(1, x + 1)
    grad_block(1, x + 3)
    gred[1].near()
    got(dpr, s_dp)
    d_own = nt(full[1, 0, own_rows], wts[1, 0]) + nt(full[1, 1, own_rows], wts[1, 1])
    dhid[own_rows] = ((d_own + dpr[...]) * slope[...]).astype(BF16)
    send(dhid.at[own_rows], dhid.at[own_rows], s_dh, partner)
    ored[0].middle()
    gred[1].middle()
    got(dhid.at[other_rows], s_dh)
    out_block(1, y + 2)
    ored[1].far()
    grad_block(0, x + 2)
    gred[0].far()
    out_block(1, y + 1)
    out_block(1, y + 3)
    ored[1].near()
    grad_block(0, x + 1)
    grad_block(0, x + 3)
    gred[0].near()
    out_block(0, y)
    grad_block(1, x)

    ones = jnp.ones((16, 768), BF16)
    terms = [nn(ones, dhid[...]), nn(ones, full[1, 0]), nn(ones, full[1, 1])]
    bt[...] = jnp.zeros_like(bt)
    for n in range(15):
        term = terms[n // 5][0:1, (n % 5) * 128 : (n % 5 + 1) * 128] * scale
        bt[n : n + 1] = term.astype(BF16).astype(F32)
    s_bt = new(8)
    for a in range(4):
        for b in range(2):
            if (a, b) != (0, 0):
                n = a * 2 + b
                send(bt, br.at[n], s_bt + n, dep_at(a, b))

    s_oz = [new(4), new(4)]

    def out_z(n):
        for i in range(2):
            xsum[n, i] = ored[n].total(i).astype(BF16)
            for kk in range(2):
                send_maybe(
                    xsum.at[n, i, pl.ds(kk * 96, 96)], zr.at[n, h], s_oz[n] + h, 2 * k + i, kk, y
                )

    s_gz, s_gr = [new(1), new(1)], [new(2), new(2)]

    def grad_zl(n):
        for i in range(2):
            gsum[n, i] = gred[n].total(i)
        gz[n, 0] = gsum[n, :, rows((1 - zl) * 80, 80)].astype(BF16)
        send(gz.at[n, 0], gz.at[n, 1], s_gz[n], zpeer)

    def grad_home(n):
        got(gz.at[n, 1], s_gz[n])
        gfin[n] = (gsum[n, :, rows(zl * 80, 80)] + gz[n, 1].astype(F32)).astype(BF16)
        for i in range(2):
            if n == 0:
                send_maybe(
                    gfin.at[0, i],
                    gu_out.at[rows(dd * 80, 80), pl.ds(pl.multiple_of(lax.rem(y, 2) * 640, 128), 640)],
                    s_gr[0] + lax.rem(y, 2), h, y // 2, 2 * k + i,
                )
            else:
                send_maybe(
                    gfin.at[1, i], rd.at[lax.rem(y, 2)], s_gr[1] + lax.rem(y, 2), 2 * k + i, y // 2, h
                )

    grad_zl(1)
    ored[1].middle()
    gred[0].middle()
    grad_home(1)
    out_block(1, y)
    grad_block(0, x)
    out_z(0)

    s_rd = new(1)
    s_gzl = [new(1), new(1)]
    for j in range(2):
        got(rd.at[j], s_gr[1] + j)
        mine, theirs = split_lanes(rd[j].astype(F32))
        gd_out[2 * k + j, rows(dd * 80, 80)] = mine.astype(BF16)
        rds[j] = theirs.astype(BF16)
    send(rds, rdo, s_rd, partner)
    got(rdo, s_rd)
    for j in range(2):
        gd_out[2 * (1 - k) + j, rows(dd * 80, 80)] = rdo[j]

    def grad_views(n):
        if n == 0:
            return lambda i, start, size: gu_out.at[rows(start, size), pl.ds(i * 640, 640)]
        return lambda i, start, size: gd_out.at[pl.ds(i * 2, 2), rows(start, size)]

    def back_zl(n):
        view = grad_views(n)
        for i in range(2):
            mine = view(i, dd * 80, 80)
            send(mine, mine, s_gb[n] + i, zpeer)

    class GatherBack(Gather):
        def __init__(self, n):
            self.p, self.right, self.left = ring("x")
            view = grad_views(n)
            self.view = lambda i, q: view(i, lax.rem(q, 4) * 160, 160)
            self.s_right, self.s_left, self.s_fwd = new(2), new(2), new(2)

    def back_first(n):
        view = grad_views(n)
        for i in range(2):
            got(view(i, (x * 2 + 1 - zl) * 80, 80), s_gb[n] + i)
            back[n].first(i)

    s_gb = [new(2), new(2)]
    back = [GatherBack(n) for n in range(2)]
    back_zl(1)
    grad_zl(0)
    grad_home(0)
    back_first(1)
    for i in range(2):
        got(gu_out.at[rows(dd * 80, 80), pl.ds(i * 640, 640)], s_gr[0] + i)
    back_zl(0)
    for i in range(2):
        back[1].forward(i)
    out_z(1)
    back_first(0)

    total = bt[...]
    for n in range(1, 8):
        got(br.at[n], s_bt + n)
        total = total + br[n]
    yb[y] = total
    s_yb = new(4)
    for a in range(1, 4):
        send(yb.at[y], yb.at[y], s_yb + a, y_at(a))
    s_pb = new(1)
    send(yb.at[y], pb, s_pb, partner)

    s_of = [new(1), new(1)]
    for n in range(2):
        total = jnp.zeros((96, 640), F32)
        for a in range(4):
            got(zr.at[n, a], s_oz[n] + a)
            total = total + zr[n, a].astype(F32)
        mine, theirs = split_lanes(total)
        osend[n] = theirs
        send(osend.at[n], orecv.at[n], s_of[n], partner)
        if n == 0:
            o_out[rows(k * 96, 96)] = (mine + bd_in[...]).astype(BF16)
        else:
            gi_out[rows(k * 96, 96)] = mine.astype(BF16)
    got(orecv.at[0], s_of[0])
    o_out[rows((1 - k) * 96, 96)] = (orecv[0] + bd_in[...]).astype(BF16)
    got(orecv.at[1], s_of[1])
    gi_out[rows((1 - k) * 96, 96)] = orecv[1].astype(BF16)

    for i in range(2):
        back[0].forward(i)
    for a in range(1, 4):
        got(yb.at[lax.rem(y + 4 - a, 4)], s_yb + a)
    got(pb, s_pb)
    bu_out[0:5] = yb[2 * k][0:5]
    bu_out[5:10] = yb[2 * k + 1][0:5]
    bd_out[0:10] = jnp.where(k == hh, yb[y][5:15], pb[5:15])
    back[1].finish()
    back[0].finish()

    for copy, when in sent:
        if when is None:
            copy.wait_send()
        else:

            @pl.when(when)
            def _(copy=copy):
                copy.wait_send()

    assert used[0] <= N_SEMS, used[0]


def per_device(tokens, up_weight, up_bias, down_weight, down_bias, out_grad):
    token_rows = tokens.shape[0]
    scale = 1.0 / math.sqrt(token_rows * lax.axis_size("col") * lax.axis_size("depth"))
    vmem = pl.BlockSpec(memory_space=pltpu.VMEM)
    hbm = pl.BlockSpec(memory_space=pl.ANY)
    scratch = [
        ((2, 96, 320), BF16),
        ((2, 96, 640), BF16),
        ((2, 80, 320), BF16),
        ((2, 80, 320), BF16),
        ((2, 80, 640), BF16),
        ((8, 1280), F32),
        ((8, 1280), F32),
        ((2, 2, 768, 640), BF16),
        ((2, 2, 640, 640), BF16),
        ((2, 640, 768), BF16),
        ((384, 640), F32),
        ((384, 640), F32),
        ((384, 640), F32),
        ((384, 640), F32),
        ((768, 640), BF16),
        ((640, 768), BF16),
        ((384, 640), F32),
        ((384, 640), F32),
        ((768, 640), BF16),
        ((2, 2, 768, 640), BF16),
        ((2, 2, 192, 640), BF16),
        ((2, 2, 2, 192, 640), BF16),
        ((2, 2, 192, 640), BF16),
        ((2, 4, 96, 640), BF16),
        ((2, 96, 320), F32),
        ((2, 96, 320), F32),
        ((2, 2, 640, 640), BF16),
        ((2, 2, 160, 640), BF16),
        ((2, 2, 2, 160, 640), BF16),
        ((2, 2, 160, 640), F32),
        ((2, 2, 2, 80, 640), BF16),
        ((2, 2, 80, 640), BF16),
        ((2, 80, 640), BF16),
        ((2, 80, 320), BF16),
        ((2, 80, 320), BF16),
        ((16, 128), F32),
        ((8, 16, 128), F32),
        ((4, 16, 128), F32),
        ((16, 128), F32),
    ]
    out = pl.pallas_call(
        lambda *refs: kernel(scale, *refs),
        name="mlp_block",
        out_shape=[
            jax.ShapeDtypeStruct((192, 320), BF16),
            jax.ShapeDtypeStruct((192, 320), BF16),
            jax.ShapeDtypeStruct((640, 1280), BF16),
            jax.ShapeDtypeStruct((4, 640, 320), BF16),
            jax.ShapeDtypeStruct((16, 128), F32),
            jax.ShapeDtypeStruct((16, 128), F32),
        ],
        in_specs=[vmem, hbm, vmem, hbm, vmem, vmem],
        out_specs=[vmem] * 6,
        scratch_shapes=[pltpu.VMEM(*s) for s in scratch] + [pltpu.SemaphoreType.DMA((N_SEMS,))],
        compiler_params=pltpu.CompilerParams(
            collective_id=0, has_side_effects=True, vmem_limit_bytes=56 << 20
        ),
        cost_estimate=pl.CostEstimate(
            flops=6 * 2 * 768 * 1280 * 640, bytes_accessed=12 << 20, transcendentals=384 * 640
        ),
    )(
        tokens,
        up_weight,
        up_bias.reshape(1, 1280),
        down_weight.reshape(4, 640, 320),
        down_bias.reshape(1, 320),
        out_grad,
    )
    layer_out, grad_in, grad_up, grad_down, bu, bd = out
    row = lax.axis_index("row")
    grad_up_bias = bu[:10].reshape(1280).astype(BF16)
    start = lax.rem(row // 2, 2) * 640 + lax.rem(row, 2) * 320
    grad_down_bias = lax.dynamic_slice(bd[:10].reshape(1280), (start,), (320,)).astype(BF16)
    return (layer_out, grad_in, grad_up, grad_up_bias, grad_down.reshape(2560, 320), grad_down_bias)


def solution(mesh):
    return jax.shard_map(
        per_device,
        mesh=mesh,
        in_specs=(
            P(("col", "depth"), "row"),
            P("col", "row"),
            P("row"),
            P("col", "row"),
            P("row"),
            P(("col", "depth"), "row"),
        ),
        out_specs=(
            P(("col", "depth"), "row"),
            P(("col", "depth"), "row"),
            P("col", "row"),
            P("row"),
            P("col", "row"),
            P("row"),
        ),
        check_vma=False,
    )
```

```python
import math

import jax
import jax.numpy as jnp
from jax import lax
from jax.experimental import pallas as pl
from jax.experimental.pallas import tpu as pltpu
from jax.sharding import PartitionSpec as P

GELU_C = math.sqrt(2.0 / math.pi)
MESH = pl.DeviceIdType.MESH
F32 = jnp.float32
BF16 = jnp.bfloat16
N_SEMS = 320


def gelu_parts(v):
    t = jnp.tanh(GELU_C * (v + 0.044715 * v * v * v))
    value = 0.5 * v * (1.0 + t)
    slope = 0.5 * (1.0 + t) + 0.5 * v * (1.0 - t * t) * GELU_C * (1.0 + 3.0 * 0.044715 * v * v)
    return value, slope


def nn(a, b):
    return lax.dot_general(a, b, (((1,), (0,)), ((), ())), preferred_element_type=F32)


def nt(a, b):
    return lax.dot_general(a, b, (((1,), (1,)), ((), ())), preferred_element_type=F32)


def rows(start, size, tile=16):
    return pl.ds(pl.multiple_of(start, tile), size)


def kernel(
    scale,
    tok, wu_in, bu_in, wd_in, bd_in, grad,
    o_out, gi_out, gu_out, gd_out, bu_out, bd_out,
    xr, piece, bb, bbr,
    full, wts, full_t,
    hps, hpr, hpo, slope, act, dhid,
    part, ra, rb, xsum, zr, osend, orecv,
    gpart, ga, gb, gz, gfin,
    bt, br, yb, pb,
    sems,
):
    row, y, dep = lax.axis_index("row"), lax.axis_index("col"), lax.axis_index("depth")
    h, k = row // 2, lax.rem(row, 2)
    zl, x = dep // 4, lax.rem(dep, 4)
    hh = h // 2
    hi = lax.rem(h, 2)

    def at(h_, k_, y_):
        return (h_ * 2 + k_, y_, dep)

    def dep_at(a, b):
        return (row, y, lax.rem(zl + b, 2) * 4 + lax.rem(x + a, 4))

    def y_at(a):
        return (row, lax.rem(y + a, 4), dep)

    partner = (h * 2 + 1 - k, y, dep)
    zpeer = dep_at(0, 1)

    bar = pltpu.get_barrier_semaphore()
    fixed = [partner] + [y_at(a) for a in (1, 2, 3)]
    fixed += [dep_at(a, b) for a in range(4) for b in range(2) if (a, b) != (0, 0)]
    for target in fixed:
        pl.semaphore_signal(bar, inc=1, device_id=target, device_id_type=MESH)
    count = len(fixed)

    def greet(h_, k_, y_):
        other = jnp.logical_not((h_ == h) & (k_ == k) & (y_ == y))

        @pl.when(other)
        def _():
            pl.semaphore_signal(bar, inc=1, device_id=at(h_, k_, y_), device_id_type=MESH)

        return other.astype(jnp.int32)

    for a in range(4):
        count = count + greet(a, hh, y)
        count = count + greet(y, hh, a)
    for a in range(2):
        for b in range(2):
            count = count + greet(2 * k + a, b, y)
            count = count + greet(2 * k + a, b, h)
        count = count + greet(h, y // 2, 2 * k + a)
    pl.semaphore_wait(bar, count)

    used = [0]
    sent = []

    def new(n=1):
        first = used[0]
        used[0] += n
        return first

    def send(src, dst, rsem, target):
        copy = pltpu.make_async_remote_copy(
            src_ref=src, dst_ref=dst, send_sem=sems.at[new()], recv_sem=sems.at[rsem],
            device_id=target, device_id_type=MESH,
        )
        copy.start()
        sent.append((copy, None))

    def send_maybe(src, dst, rsem, h_, k_, y_):
        mine = (h_ == h) & (k_ == k) & (y_ == y)
        copy = pltpu.make_async_remote_copy(
            src_ref=src, dst_ref=dst, send_sem=sems.at[new()], recv_sem=sems.at[rsem],
            device_id=at(h_, k_, y_), device_id_type=MESH,
        )

        @pl.when(jnp.logical_not(mine))
        def _():
            copy.start()

        @pl.when(mine)
        def _():
            pltpu.make_async_copy(src, dst, sems.at[rsem]).start()

        sent.append((copy, jnp.logical_not(mine)))

    def got(dst, rsem):
        pltpu.make_async_copy(dst, dst, sems.at[rsem]).wait()

    def chunk(buf):
        return lambda i, q: buf.at[i, :, rows(lax.rem(q, 4) * 80, 80)]

    def token_rows(buf):
        return lambda i, q: buf.at[i, rows(lax.rem(q, 4) * 192, 192)]

    def ring(axis):
        if axis == "y":
            return y, y_at(1), y_at(3)
        return x, dep_at(1, 0), dep_at(3, 0)

    class Gather:
        def __init__(self, view, axis):
            self.p, self.right, self.left = ring(axis)
            self.view = view
            self.s_right, self.s_left, self.s_fwd = new(2), new(2), new(2)

        def first(self, i):
            mine = self.view(i, self.p)
            pair = [(self.s_right + i, self.right), (self.s_left + i, self.left)]
            for sem, target in pair if i == 0 else pair[::-1]:
                send(mine, mine, sem, target)

        def forward(self, i):
            if i == 0:
                block = self.view(0, self.p + 3)
                got(block, self.s_right)
                send(block, block, self.s_fwd, self.right)
            else:
                block = self.view(1, self.p + 1)
                got(block, self.s_left + 1)
                send(block, block, self.s_fwd + 1, self.left)

        def finish(self):
            got(self.view(1, self.p + 3), self.s_right + 1)
            got(self.view(0, self.p + 1), self.s_left)
            got(self.view(0, self.p + 2), self.s_fwd)
            got(self.view(1, self.p + 2), self.s_fwd + 1)

    class Reduce:
        def __init__(self, view, first, second, axis):
            self.p, self.right, self.left = ring(axis)
            self.view = view
            self.first, self.second = first, second
            self.s1, self.s2 = new(2), new(4)

        def far(self):
            send(self.view(0, self.p + 2), self.first.at[0], self.s1, self.right)
            send(self.view(1, self.p + 2), self.first.at[1], self.s1 + 1, self.left)

        def near(self):
            send(self.view(1, self.p + 1), self.second.at[0, 1], self.s2 + 1, self.right)
            send(self.view(0, self.p + 3), self.second.at[1, 0], self.s2 + 2, self.left)

        def middle(self):
            for i, q, target in ((0, self.p + 1, self.right), (1, self.p + 3, self.left)):
                got(self.first.at[i], self.s1 + i)
                block = self.view(i, q)
                block[...] = (block[...].astype(F32) + self.first[i].astype(F32)).astype(BF16)
                send(block, self.second.at[i, i], self.s2 + 3 * i, target)

        def total(self, i):
            got(self.second.at[0, i], self.s2 + i)
            got(self.second.at[1, i], self.s2 + 2 + i)
            return (
                self.view(i, self.p)[...].astype(F32)
                + self.second[0, i].astype(F32)
                + self.second[1, i].astype(F32)
            )

    def pair_lanes(own, other):
        first = jnp.where(k == 0, own, other).astype(F32)
        second = jnp.where(k == 0, other, own).astype(F32)
        return jnp.concatenate([first, second], axis=1).astype(BF16)

    def split_lanes(both):
        low, high = both[:, :320], both[:, 320:]
        return jnp.where(k == 0, low, high), jnp.where(k == 0, high, low)

    s_x = new(2)
    for n, src in enumerate((tok, grad)):
        send(src.at[rows((1 - k) * 96, 96)], xr.at[n], s_x + n, partner)
    quarter = rows(x * 80, 80)
    s_w = [new(2), new(4)]
    for j in range(2):
        send_maybe(
            wu_in.at[:, quarter, pl.ds(j * 640, 640)],
            wts.at[0, lax.rem(y, 2), :, quarter],
            s_w[0] + lax.rem(y, 2), h, y // 2, 2 * k + j,
        )
    bb[...] = jnp.broadcast_to(bu_in[...], bb.shape)
    s_bb = new(1)
    send(bb, bbr, s_bb, partner)

    s_piece = [new(4), new(4)]

    def send_piece(n, src):
        got(xr.at[n], s_x + n)
        piece[n] = pair_lanes(src[rows(k * 96, 96), :], xr[n])
        for a in range(4):
            send_maybe(
                piece.at[n],
                full.at[n, hi, rows(y * 192 + k * 96, 96)],
                s_piece[n] + hi * 2 + k, lax.rem(h + a, 4), hh, y,
            )

    def got_pieces(n, i):
        for kk in range(2):
            got(full.at[n, i, rows(y * 192 + kk * 96, 96)], s_piece[n] + i * 2 + kk)

    send_piece(0, tok)
    for j in range(4):
        send_maybe(
            wd_in.at[quarter, pl.ds(j * 640, 640)],
            wts.at[1, hi, k, quarter],
            s_w[1] + hi * 2 + k, y, hh, j,
        )
    send_piece(1, grad)

    wag = [Gather(chunk(wts.at[n]), "x") for n in range(2)]
    tag = [Gather(token_rows(full.at[n]), "y") for n in range(2)]

    for i in range(2):
        got(wts.at[0, i, :, quarter], s_w[0] + i)
        wag[0].first(i)
    for i in range(2):
        got_pieces(0, i)
        tag[0].first(i)
    for i in range(2):
        wag[0].forward(i)
    for i in range(2):
        tag[0].forward(i)
    for i in range(2):
        for kk in range(2):
            got(wts.at[1, i, kk, quarter], s_w[1] + i * 2 + kk)
        wag[1].first(i)
    for i in range(2):
        got_pieces(1, i)
        tag[1].first(i)

    half = 384
    own_rows = rows(k * half, half)
    other_rows = rows((1 - k) * half, half)

    def weight(n, i):
        return wts[n, i].reshape(640, 640)

    def hidden(n, block):
        return nn(full[n, 0, block], weight(n, 0)) + nn(full[n, 1, block], weight(n, 1))

    def transpose(n):
        for i in range(2):
            full_t[n, i] = full[n, i].T.reshape(2, 320, 768)

    s_hp, s_act = [new(1), new(1)], [new(1), new(1)]
    tag[0].finish()
    wag[0].finish()
    hps[0] = hidden(0, other_rows)
    send(hps.at[0], hpr.at[0], s_hp[0], partner)
    hpo[...] = hidden(0, own_rows)
    for i in range(2):
        wag[1].forward(i)
    for i in range(2):
        tag[1].forward(i)
    transpose(0)
    got(bbr, s_bb)
    low = jnp.where(k == y // 2, bb[0:1], bbr[0:1])
    bias = jnp.where(lax.rem(y, 2) == 0, low[:, :640], low[:, 640:])
    got(hpr.at[0], s_hp[0])
    value, slope_now = gelu_parts(hpo[...] + hpr[0] + bias)
    slope[...] = slope_now
    act[own_rows] = value.astype(BF16)
    send(act.at[own_rows], act.at[own_rows], s_act[0], partner)

    tag[1].finish()
    transpose(1)
    wag[1].finish()
    hps[1] = hidden(1, other_rows)
    send(hps.at[1], hpr.at[1], s_hp[1], partner)
    got(act.at[other_rows], s_act[0])

    ored = [Reduce(token_rows(part.at[n]), ra.at[n], rb.at[n], "y") for n in range(2)]
    gred = [Reduce(chunk(gpart.at[n]), ga.at[n], gb.at[n], "x") for n in range(2)]

    def out_block(n, q):
        block = rows(lax.rem(q, 4) * 192, 192)
        left = act if n == 0 else dhid
        for i in range(2):
            part[n, i, block] = nt(left[block], weight(1 - n, i)).astype(BF16)

    def grad_block(n, q):
        block = rows(lax.rem(q, 4) * 80, 80)
        right = dhid if n == 0 else act
        for i in range(2):
            left = full_t[n, i, :, block].reshape(160, 768)
            gpart[n, i, :, block] = (nn(left, right[...]) * scale).astype(BF16).reshape(2, 80, 640)

    grad_block(1, x + 2)
    gred[1].far()
    out_block(0, y + 2)
    ored[0].far()
    grad_block(1, x + 1)
    grad_block(1, x + 3)
    gred[1].near()
    out_block(0, y + 1)
    out_block(0, y + 3)
    ored[0].near()
    d_own = hidden(1, own_rows)
    got(hpr.at[1], s_hp[1])
    dhid[own_rows] = ((d_own + hpr[1]) * slope[...]).astype(BF16)
    send(dhid.at[own_rows], dhid.at[own_rows], s_act[1], partner)
    grad_block(1, x)
    gred[1].middle()
    got(dhid.at[other_rows], s_act[1])
    grad_block(0, x + 2)
    gred[0].far()
    ored[0].middle()
    out_block(1, y + 2)
    ored[1].far()
    grad_block(0, x + 1)
    grad_block(0, x + 3)
    gred[0].near()
    out_block(1, y + 1)
    out_block(1, y + 3)
    ored[1].near()
    grad_block(0, x)
    out_block(0, y)
    out_block(1, y)

    ones = jnp.ones((16, 768), BF16)
    terms = [nn(ones, dhid[...]), nn(ones, full[1, 0]), nn(ones, full[1, 1])]
    bt[...] = jnp.zeros_like(bt)
    for n in range(15):
        term = terms[n // 5][0:1, (n % 5) * 128 : (n % 5 + 1) * 128] * scale
        bt[n : n + 1] = term.astype(BF16).astype(F32)
    br[dep] = bt[...]
    s_bt = new(8)
    for a in range(4):
        for b in range(2):
            if (a, b) != (0, 0):
                send(bt, br.at[dep], s_bt + a * 2 + b, dep_at(a, b))

    s_oz = [new(4), new(4)]

    def out_z(n):
        for i in range(2):
            xsum[n, i] = ored[n].total(i).astype(BF16)
            for kk in range(2):
                send_maybe(
                    xsum.at[n, i, pl.ds(kk * 96, 96)], zr.at[n, h], s_oz[n] + h, 2 * k + i, kk, y
                )

    s_gz, s_gr = [new(2), new(2)], [new(2), new(4)]

    def grad_zl(n):
        for i in range(2):
            gz[n, 0, i] = gred[n].total(i).astype(BF16)
            send(gz.at[n, 0, i], gz.at[n, 1, i], s_gz[n] + i, zpeer)

    def grad_home(n):
        for i in range(2):
            got(gz.at[n, 1, i], s_gz[n] + i)
            gfin[n, i] = (gz[n, 0, i].astype(F32) + gz[n, 1, i].astype(F32)).astype(BF16)
            if n == 0:
                lanes = pl.ds(pl.multiple_of(lax.rem(y, 2) * 640, 128), 640)
                send_maybe(
                    gfin.at[0, i], gu_out.at[:, quarter, lanes],
                    s_gr[0] + lax.rem(y, 2), h, y // 2, 2 * k + i,
                )
            else:
                lanes = pl.ds(pl.multiple_of(y * 640, 128), 640)
                for kk in range(2):
                    send_maybe(
                        gfin.at[1, i, kk], gd_out.at[quarter, lanes], s_gr[1] + y, 2 * k + i, kk, h
                    )

    back = [
        Gather(lambda i, q: gu_out.at[:, rows(lax.rem(q, 4) * 80, 80), pl.ds(i * 640, 640)], "x"),
        Gather(lambda i, q: gd_out.at[rows(lax.rem(q, 4) * 80, 80), pl.ds(i * 1280, 1280)], "x"),
    ]

    def back_first(n):
        for i in range(2):
            if n == 0:
                got(gu_out.at[:, quarter, pl.ds(i * 640, 640)], s_gr[0] + i)
            else:
                for j in range(2):
                    got(gd_out.at[quarter, pl.ds((2 * i + j) * 640, 640)], s_gr[1] + 2 * i + j)
            back[n].first(i)

    s_of = [new(1), new(1)]

    def out_last(n):
        total = jnp.zeros((96, 640), F32)
        for a in range(4):
            got(zr.at[n, a], s_oz[n] + a)
            total = total + zr[n, a].astype(F32)
        mine, theirs = split_lanes(total)
        osend[n] = theirs
        send(osend.at[n], orecv.at[n], s_of[n], partner)
        if n == 0:
            o_out[rows(k * 96, 96)] = (mine + bd_in[...]).astype(BF16)
        else:
            gi_out[rows(k * 96, 96)] = mine.astype(BF16)

    grad_zl(1)
    gred[0].middle()
    ored[1].middle()
    grad_home(1)
    out_z(0)
    grad_zl(0)
    back_first(1)
    out_z(1)
    grad_home(0)

    for a in range(4):
        for b in range(2):
            if (a, b) != (0, 0):
                from_dep = lax.rem(zl + b, 2) * 4 + lax.rem(x + 4 - a, 4)
                got(br.at[from_dep], s_bt + a * 2 + b)
    total = br[0]
    for n in range(1, 8):
        total = total + br[n]
    yb[y] = total
    s_yb = new(4)
    for a in range(1, 4):
        send(yb.at[y], yb.at[y], s_yb + a, y_at(a))
    s_pb = new(1)
    send(yb.at[y], pb, s_pb, partner)

    for i in range(2):
        back[1].forward(i)
    back_first(0)
    out_last(0)
    for i in range(2):
        back[0].forward(i)
    out_last(1)
    got(orecv.at[0], s_of[0])
    o_out[rows((1 - k) * 96, 96)] = (orecv[0] + bd_in[...]).astype(BF16)
    for a in range(1, 4):
        got(yb.at[lax.rem(y + 4 - a, 4)], s_yb + a)
    got(pb, s_pb)
    bu_out[0:5] = yb[2 * k][0:5]
    bu_out[5:10] = yb[2 * k + 1][0:5]
    bd_out[0:10] = jnp.where(k == hh, yb[y][5:15], pb[5:15])
    got(orecv.at[1], s_of[1])
    gi_out[rows((1 - k) * 96, 96)] = orecv[1].astype(BF16)
    back[1].finish()
    back[0].finish()

    for copy, when in sent:
        if when is None:
            copy.wait_send()
        else:

            @pl.when(when)
            def _(copy=copy):
                copy.wait_send()

    assert used[0] <= N_SEMS, used[0]


def per_device(tokens, up_weight, up_bias, down_weight, down_bias, out_grad):
    token_rows = tokens.shape[0]
    scale = 1.0 / math.sqrt(token_rows * lax.axis_size("col") * lax.axis_size("depth"))
    vmem = pl.BlockSpec(memory_space=pltpu.VMEM)
    hbm = pl.BlockSpec(memory_space=pl.ANY)
    scratch = [
        ((2, 96, 320), BF16),
        ((2, 96, 640), BF16),
        ((8, 1280), F32),
        ((8, 1280), F32),
        ((2, 2, 768, 640), BF16),
        ((2, 2, 2, 320, 640), BF16),
        ((2, 2, 2, 320, 768), BF16),
        ((2, 384, 640), F32),
        ((2, 384, 640), F32),
        ((384, 640), F32),
        ((384, 640), F32),
        ((768, 640), BF16),
        ((768, 640), BF16),
        ((2, 2, 768, 640), BF16),
        ((2, 2, 192, 640), BF16),
        ((2, 2, 2, 192, 640), BF16),
        ((2, 2, 192, 640), BF16),
        ((2, 4, 96, 640), BF16),
        ((2, 96, 320), F32),
        ((2, 96, 320), F32),
        ((2, 2, 2, 320, 640), BF16),
        ((2, 2, 2, 80, 640), BF16),
        ((2, 2, 2, 2, 80, 640), BF16),
        ((2, 2, 2, 2, 80, 640), BF16),
        ((2, 2, 2, 80, 640), BF16),
        ((16, 128), F32),
        ((8, 16, 128), F32),
        ((4, 16, 128), F32),
        ((16, 128), F32),
    ]
    out = pl.pallas_call(
        lambda *refs: kernel(scale, *refs),
        name="mlp_block",
        out_shape=[
            jax.ShapeDtypeStruct((192, 320), BF16),
            jax.ShapeDtypeStruct((192, 320), BF16),
            jax.ShapeDtypeStruct((2, 320, 1280), BF16),
            jax.ShapeDtypeStruct((320, 2560), BF16),
            jax.ShapeDtypeStruct((16, 128), F32),
            jax.ShapeDtypeStruct((16, 128), F32),
        ],
        in_specs=[vmem, hbm, vmem, hbm, vmem, vmem],
        out_specs=[vmem] * 6,
        scratch_shapes=[pltpu.VMEM(*s) for s in scratch] + [pltpu.SemaphoreType.DMA((N_SEMS,))],
        compiler_params=pltpu.CompilerParams(
            collective_id=0, has_side_effects=True, vmem_limit_bytes=56 << 20
        ),
        cost_estimate=pl.CostEstimate(
            flops=6 * 2 * 768 * 1280 * 640, bytes_accessed=12 << 20, transcendentals=384 * 640
        ),
    )(
        tokens,
        up_weight.reshape(2, 320, 1280),
        up_bias.reshape(1, 1280),
        down_weight.T,
        down_bias.reshape(1, 320),
        out_grad,
    )
    layer_out, grad_in, grad_up, grad_down, bu, bd = out
    row = lax.axis_index("row")
    grad_up_bias = bu[:10].reshape(1280).astype(BF16)
    start = lax.rem(row // 2, 2) * 640 + lax.rem(row, 2) * 320
    grad_down_bias = lax.dynamic_slice(bd[:10].reshape(1280), (start,), (320,)).astype(BF16)
    grad_up = grad_up.reshape(640, 1280)
    return (layer_out, grad_in, grad_up, grad_up_bias, grad_down.T, grad_down_bias)


def solution(mesh):
    return jax.shard_map(
        per_device,
        mesh=mesh,
        in_specs=(
            P(("col", "depth"), "row"),
            P("col", "row"),
            P("row"),
            P("col", "row"),
            P("row"),
            P(("col", "depth"), "row"),
        ),
        out_specs=(
            P(("col", "depth"), "row"),
            P(("col", "depth"), "row"),
            P("col", "row"),
            P("row"),
            P("col", "row"),
            P("row"),
        ),
        check_vma=False,
    )
```

```python
import math

import jax
import jax.numpy as jnp
from jax import lax
from jax.experimental import pallas as pl
from jax.experimental.pallas import tpu as pltpu
from jax.sharding import PartitionSpec as P

GELU_C = math.sqrt(2.0 / math.pi)
MESH = pl.DeviceIdType.MESH
F32 = jnp.float32
BF16 = jnp.bfloat16
N_SEMS = 320


def gelu_parts(v):
    t = jnp.tanh(GELU_C * (v + 0.044715 * v * v * v))
    value = 0.5 * v * (1.0 + t)
    slope = 0.5 * (1.0 + t) + 0.5 * v * (1.0 - t * t) * GELU_C * (1.0 + 3.0 * 0.044715 * v * v)
    return value, slope


def nn(a, b):
    return lax.dot_general(a, b, (((1,), (0,)), ((), ())), preferred_element_type=F32)


def nt(a, b):
    return lax.dot_general(a, b, (((1,), (1,)), ((), ())), preferred_element_type=F32)


def rows(start, size, tile=16):
    return pl.ds(pl.multiple_of(start, tile), size)


def kernel(
    scale,
    tok, wu_in, bu_in, wd_in, bd_in, grad,
    o_out, gi_out, gu_out, gd_out, bu_out, bd_out,
    xr, piece, wq, bb, bbr,
    full, wts, full_t,
    hps, hpr, hpo, slope, act, dhid,
    part, ra, rb, xsum, zr, osend, orecv,
    gpart, ga, gb, gsum, gs, gz, gfin,
    bt, br, yb, pb,
    sems,
):
    row, y, dep = lax.axis_index("row"), lax.axis_index("col"), lax.axis_index("depth")
    h, k = row // 2, lax.rem(row, 2)
    zl, x = dep // 4, lax.rem(dep, 4)
    hh = h // 2
    hi = lax.rem(h, 2)

    def at(h_, k_, y_, plane):
        return (h_ * 2 + k_, y_, plane * 4 + x)

    def is_me(h_, k_, y_, plane):
        return (h_ == h) & (k_ == k) & (y_ == y) & (plane == zl)

    def z_at(a):
        return (lax.rem(h + a, 4) * 2 + k, y, dep)

    def dep_at(a, b):
        return (row, y, lax.rem(zl + b, 2) * 4 + lax.rem(x + a, 4))

    def y_at(a):
        return (row, lax.rem(y + a, 4), dep)

    partner = (h * 2 + 1 - k, y, dep)
    zpeer = dep_at(0, 1)

    bar = pltpu.get_barrier_semaphore()
    fixed = [partner, z_at(1), z_at(3)] + [y_at(a) for a in (1, 2, 3)]
    fixed += [dep_at(a, b) for a in range(4) for b in range(2) if (a, b) != (0, 0)]
    for target in fixed:
        pl.semaphore_signal(bar, inc=1, device_id=target, device_id_type=MESH)
    count = len(fixed)

    def greet(*place):
        other = jnp.logical_not(is_me(*place))

        @pl.when(other)
        def _():
            pl.semaphore_signal(bar, inc=1, device_id=at(*place), device_id_type=MESH)

        return other.astype(jnp.int32)

    for a in range(4):
        count = count + greet(a, hh, y, zl)
        count = count + greet(y, hh, a, k)
    for a in range(2):
        for b in range(2):
            count = count + greet(2 * k + a, b, y, zl)
            count = count + greet(2 * k + a, zl, h, b)
            count = count + greet(h, y // 2, 2 * k + a, b)
    pl.semaphore_wait(bar, count)

    used = [0]
    sent = []

    def new(n=1):
        first = used[0]
        used[0] += n
        return first

    def send(src, dst, rsem, target):
        copy = pltpu.make_async_remote_copy(
            src_ref=src, dst_ref=dst, send_sem=sems.at[new()], recv_sem=sems.at[rsem],
            device_id=target, device_id_type=MESH,
        )
        copy.start()
        sent.append((copy, None))

    def send_if(only, src, dst, rsem, *place):
        mine = is_me(*place)
        away = jnp.logical_not(mine) & only
        copy = pltpu.make_async_remote_copy(
            src_ref=src, dst_ref=dst, send_sem=sems.at[new()], recv_sem=sems.at[rsem],
            device_id=at(*place), device_id_type=MESH,
        )

        @pl.when(away)
        def _():
            copy.start()

        @pl.when(mine & only)
        def _():
            pltpu.make_async_copy(src, dst, sems.at[rsem]).start()

        sent.append((copy, away))

    def got(dst, rsem):
        pltpu.make_async_copy(dst, dst, sems.at[rsem]).wait()

    def got_if(only, dst, rsem):
        @pl.when(only)
        def _():
            got(dst, rsem)

    def token_view(buf):
        return lambda i, q: buf.at[i, rows(lax.rem(q, 4) * 192, 192)]

    def half_view(buf, i):
        return lambda kk, q: buf.at[i, rows(lax.rem(q, 4) * 192 + kk * 96, 96)]

    def chunk_view(buf):
        return lambda i, q: buf.at[i, :, rows(lax.rem(q, 4) * 80, 80)]

    def chunk_half_view(buf, i):
        return lambda kk, q: buf.at[i, kk, rows(lax.rem(q, 4) * 80, 80)]

    def ring(axis):
        if axis == "y":
            return y, y_at(1), y_at(3)
        return x, dep_at(1, 0), dep_at(3, 0)

    class Gather:
        def __init__(self, view, axis):
            self.p, self.right, self.left = ring(axis)
            self.view = view
            self.s_right, self.s_left, self.s_fwd = new(2), new(2), new(2)

        def first(self, i):
            mine = self.view(i, self.p)
            pair = [(self.s_right + i, self.right), (self.s_left + i, self.left)]
            for sem, target in pair if i == 0 else pair[::-1]:
                send(mine, mine, sem, target)

        def forward(self, i):
            if i == 0:
                block = self.view(0, self.p + 3)
                got(block, self.s_right)
                send(block, block, self.s_fwd, self.right)
            else:
                block = self.view(1, self.p + 1)
                got(block, self.s_left + 1)
                send(block, block, self.s_fwd + 1, self.left)

        def finish(self):
            got(self.view(1, self.p + 3), self.s_right + 1)
            got(self.view(0, self.p + 1), self.s_left)
            got(self.view(0, self.p + 2), self.s_fwd)
            got(self.view(1, self.p + 2), self.s_fwd + 1)

    class Reduce:
        def __init__(self, view, first, second, axis):
            self.p, self.right, self.left = ring(axis)
            self.view = view
            self.first, self.second = first, second
            self.s1, self.s2 = new(2), new(4)

        def far(self):
            send(self.view(0, self.p + 2), self.first.at[0], self.s1, self.right)
            send(self.view(1, self.p + 2), self.first.at[1], self.s1 + 1, self.left)

        def near(self):
            send(self.view(1, self.p + 1), self.second.at[0, 1], self.s2 + 1, self.right)
            send(self.view(0, self.p + 3), self.second.at[1, 0], self.s2 + 2, self.left)

        def middle(self):
            for i, q, target in ((0, self.p + 1, self.right), (1, self.p + 3, self.left)):
                got(self.first.at[i], self.s1 + i)
                block = self.view(i, q)
                block[...] = (block[...].astype(F32) + self.first[i].astype(F32)).astype(BF16)
                send(block, self.second.at[i, i], self.s2 + 3 * i, target)

        def total(self, i):
            got(self.second.at[0, i], self.s2 + i)
            got(self.second.at[1, i], self.s2 + 2 + i)
            return (
                self.view(i, self.p)[...].astype(F32)
                + self.second[0, i].astype(F32)
                + self.second[1, i].astype(F32)
            )

    def pair_lanes(own, other):
        first = jnp.where(k == 0, own, other).astype(F32)
        second = jnp.where(k == 0, other, own).astype(F32)
        return jnp.concatenate([first, second], axis=1).astype(BF16)

    def split_lanes(both):
        low, high = both[:, :320], both[:, 320:]
        return jnp.where(k == 0, low, high), jnp.where(k == 0, high, low)

    s_x = new(2)
    for n, src in enumerate((tok, grad)):
        send(src.at[rows((1 - k) * 96, 96)], xr.at[n], s_x + n, partner)
    quarter = rows(x * 80, 80)
    always = k >= 0

    def lanes(n):
        return pl.ds(pl.multiple_of(n * 640, 128), 640)

    s_w = [new(2), new(4)]
    for j in range(2):
        send_if(
            always,
            wu_in.at[:, quarter, pl.ds(j * 640, 640)],
            wts.at[0, lax.rem(y, 2), :, quarter],
            s_w[0] + lax.rem(y, 2), h, y // 2, 2 * k + j, zl,
        )
    s_wq = new(4)
    for a in range(4):
        y_to = lax.rem(y + a, 4)
        send_if(always, wd_in.at[quarter, lanes(y_to)], wq.at[y], s_wq + a, h, k, y_to, zl)
    bb[...] = jnp.broadcast_to(bu_in[...], bb.shape)
    s_bb = new(1)
    send(bb, bbr, s_bb, partner)

    s_piece = [new(4), new(4)]
    to_right = [h == lax.rem(2 * k + i + 1, 4) for i in range(2)]
    to_left = [h == lax.rem(2 * k + i + 3, 4) for i in range(2)]

    def part_of(n, i, kk):
        return full.at[n, i, rows(y * 192 + kk * 96, 96)]

    def send_piece(n, src):
        got(xr.at[n], s_x + n)
        piece[n] = pair_lanes(src[rows(k * 96, 96), :], xr[n])
        dst = part_of(n, hi, k)
        sem = s_piece[n] + hi * 2 + k
        for a in (1, 3):
            send_if(always, piece.at[n], dst, sem, lax.rem(h + a, 4), hh, y, zl)
        send_if(always, piece.at[n], dst, sem, h, hh, y, zl)

    def pass_piece(n):
        for i in range(2):
            for kk, only, a in ((0, to_right[i], 1), (1, to_left[i], 3)):
                sem = s_piece[n] + i * 2 + kk
                block = part_of(n, i, kk)
                got_if(only, block, sem)
                send_if(only, block, block, sem, lax.rem(h + a, 4), k, y, zl)

    def got_piece(n, i, kk):
        only = (to_right, to_left)[kk][i]
        got_if(jnp.logical_not(only), part_of(n, i, kk), s_piece[n] + i * 2 + kk)

    wag = [Gather(chunk_view(wts.at[n]), "x") for n in range(2)]
    tag = [[Gather(half_view(full.at[n], i), "y") for i in range(2)] for n in range(2)]

    def over_y(n, i, kk):
        got_piece(n, i, kk)
        tag[n][i].first(kk)

    send_piece(0, tok)
    for i in range(2):
        got(wts.at[0, i, :, quarter], s_w[0] + i)
        wag[0].first(i)
    pass_piece(0)
    for a in range(4):
        origin = lax.rem(y + 4 - a, 4)
        got(wq.at[origin], s_wq + a)
        send_if(
            always, wq.at[origin], wts.at[1, hi, k, quarter], s_w[1] + hi * 2 + k, origin, hh, y, zl
        )
    for i in range(2):
        for kk in range(2):
            over_y(0, i, kk)
    send_piece(1, grad)
    for i in range(2):
        wag[0].forward(i)
    for i in range(2):
        for kk in range(2):
            tag[0][i].forward(kk)
    for i in range(2):
        for kk in range(2):
            got(wts.at[1, i, kk, quarter], s_w[1] + i * 2 + kk)
        wag[1].first(i)
    pass_piece(1)
    over_y(1, 0, 0)
    over_y(1, 0, 1)
    over_y(1, 1, 0)

    half = 384
    own_rows = rows(k * half, half)
    other_rows = rows((1 - k) * half, half)

    def weight(n, i):
        return wts[n, i].reshape(640, 640)

    def hidden(n, block):
        return nn(full[n, 0, block], weight(n, 0)) + nn(full[n, 1, block], weight(n, 1))

    def transpose(n, i):
        full_t[n, i] = full[n, i].T.reshape(2, 320, 768)

    s_hp, s_act = [new(1), new(1)], [new(1), new(1)]
    tag[0][0].finish()
    tag[0][1].finish()
    wag[0].finish()
    hps[0] = hidden(0, other_rows)
    send(hps.at[0], hpr.at[0], s_hp[0], partner)
    hpo[...] = hidden(0, own_rows)
    for kk in range(2):
        tag[1][0].forward(kk)
    over_y(1, 1, 1)
    got(bbr, s_bb)
    low = jnp.where(k == y // 2, bb[0:1], bbr[0:1])
    bias = jnp.where(lax.rem(y, 2) == 0, low[:, :640], low[:, 640:])
    got(hpr.at[0], s_hp[0])
    value, slope_now = gelu_parts(hpo[...] + hpr[0] + bias)
    slope[...] = slope_now
    act[own_rows] = value.astype(BF16)
    send(act.at[own_rows], act.at[own_rows], s_act[0], partner)
    for i in range(2):
        transpose(0, i)
    for i in range(2):
        wag[1].forward(i)
    got(act.at[other_rows], s_act[0])

    ored = [Reduce(token_view(part.at[n]), ra.at[n], rb.at[n], "y") for n in range(2)]
    gred = [
        [Reduce(chunk_half_view(gpart.at[n], i), ga.at[n, i], gb.at[n, i], "x") for i in range(2)]
        for n in range(2)
    ]

    def out_block(n, q):
        block = rows(lax.rem(q, 4) * 192, 192)
        left = act if n == 0 else dhid
        for i in range(2):
            part[n, i, block] = nt(left[block], weight(1 - n, i)).astype(BF16)

    def grad_block(n, i, q):
        block = rows(lax.rem(q, 4) * 80, 80)
        right = dhid if n == 0 else act
        left = full_t[n, i, :, block].reshape(160, 768)
        gpart[n, i, :, block] = (nn(left, right[...]) * scale).astype(BF16).reshape(2, 80, 640)

    def grad_start(n, i):
        grad_block(n, i, x + 2)
        gred[n][i].far()
        grad_block(n, i, x + 1)
        grad_block(n, i, x + 3)
        gred[n][i].near()

    def grad_middle(n, i):
        grad_block(n, i, x)
        gred[n][i].middle()

    s_oz = [new(4), new(4)]

    def out_z(n):
        for i in range(2):
            xsum[n, i] = ored[n].total(i).astype(BF16)
            for kk in range(2):
                send_if(
                    always, xsum.at[n, i, pl.ds(kk * 96, 96)], zr.at[n, h], s_oz[n] + h,
                    2 * k + i, kk, y, zl,
                )

    s_gz, s_gr = [new(2), new(2)], [new(4), new(4)]

    def grad_zl(n, i):
        for kk in range(2):
            gsum[n, i, kk] = gred[n][i].total(kk)
        gs[n, i] = gsum[n, i, 1 - zl].astype(BF16)
        send(gs.at[n, i], gz.at[n, i], s_gz[n] + i, zpeer)

    def grad_home(n, i):
        got(gz.at[n, i], s_gz[n] + i)
        gfin[n, i] = (gsum[n, i, zl] + gz[n, i].astype(F32)).astype(BF16)
        for p in range(2):
            plane = lax.rem(zl + 1 - p, 2)
            if n == 0:
                send_if(
                    always, gfin.at[0, i], gu_out.at[zl, quarter, lanes(lax.rem(y, 2))],
                    s_gr[0] + 2 * (1 - p) + lax.rem(y, 2), h, y // 2, 2 * k + i, plane,
                )
            else:
                send_if(
                    always, gfin.at[1, i], gd_out.at[quarter, lanes(y)],
                    s_gr[1] + y, 2 * k + i, zl, h, plane,
                )

    back = [
        Gather(lambda i, q: gu_out.at[:, rows(lax.rem(q, 4) * 80, 80), pl.ds(i * 640, 640)], "x"),
        Gather(lambda i, q: gd_out.at[rows(lax.rem(q, 4) * 80, 80), pl.ds(i * 1280, 1280)], "x"),
    ]

    def back_first(n):
        for i in range(2):
            if n == 0:
                got(gu_out.at[zl, quarter, pl.ds(i * 640, 640)], s_gr[0] + i)
                got(gu_out.at[1 - zl, quarter, pl.ds(i * 640, 640)], s_gr[0] + 2 + i)
            else:
                for j in range(2):
                    got(gd_out.at[quarter, pl.ds((2 * i + j) * 640, 640)], s_gr[1] + 2 * i + j)
            back[n].first(i)

    s_of = [new(1), new(1)]

    def out_last(n):
        total = jnp.zeros((96, 640), F32)
        for a in range(4):
            got(zr.at[n, a], s_oz[n] + a)
            total = total + zr[n, a].astype(F32)
        mine, theirs = split_lanes(total)
        osend[n] = theirs
        send(osend.at[n], orecv.at[n], s_of[n], partner)
        if n == 0:
            o_out[rows(k * 96, 96)] = (mine + bd_in[...]).astype(BF16)
        else:
            gi_out[rows(k * 96, 96)] = mine.astype(BF16)

    tag[1][0].finish()
    transpose(1, 0)
    grad_start(1, 0)
    for kk in range(2):
        tag[1][1].forward(kk)
    wag[1].finish()
    out_block(0, y + 2)
    ored[0].far()
    grad_middle(1, 0)
    tag[1][1].finish()
    hps[1] = hidden(1, other_rows)
    send(hps.at[1], hpr.at[1], s_hp[1], partner)
    transpose(1, 1)
    grad_start(1, 1)
    d_own = hidden(1, own_rows)
    got(hpr.at[1], s_hp[1])
    dhid[own_rows] = ((d_own + hpr[1]) * slope[...]).astype(BF16)
    send(dhid.at[own_rows], dhid.at[own_rows], s_act[1], partner)
    out_block(0, y + 1)
    out_block(0, y + 3)
    ored[0].near()
    grad_zl(1, 0)
    grad_middle(1, 1)
    got(dhid.at[other_rows], s_act[1])
    grad_start(0, 0)
    ored[0].middle()
    grad_home(1, 0)
    grad_start(0, 1)
    grad_zl(1, 1)
    out_block(1, y + 2)
    ored[1].far()
    grad_middle(0, 0)
    out_block(1, y + 1)
    out_block(1, y + 3)
    ored[1].near()
    grad_home(1, 1)
    grad_middle(0, 1)
    out_block(0, y)
    out_block(1, y)
    grad_zl(0, 0)
    ored[1].middle()
    grad_zl(0, 1)
    out_z(0)
    ones = jnp.ones((16, 768), BF16)
    terms = [nn(ones, dhid[...]), nn(ones, full[1, 0]), nn(ones, full[1, 1])]
    bt[...] = jnp.zeros_like(bt)
    for n in range(15):
        term = terms[n // 5][0:1, (n % 5) * 128 : (n % 5 + 1) * 128] * scale
        bt[n : n + 1] = term.astype(BF16).astype(F32)
    br[dep] = bt[...]
    s_bt = new(8)
    for a in range(4):
        for b in range(2):
            if (a, b) != (0, 0):
                send(bt, br.at[dep], s_bt + a * 2 + b, dep_at(a, b))

    back_first(1)
    grad_home(0, 0)
    grad_home(0, 1)
    out_z(1)

    for a in range(4):
        for b in range(2):
            if (a, b) != (0, 0):
                from_dep = lax.rem(zl + b, 2) * 4 + lax.rem(x + 4 - a, 4)
                got(br.at[from_dep], s_bt + a * 2 + b)
    total = br[0]
    for n in range(1, 8):
        total = total + br[n]
    yb[y] = total
    s_yb = new(4)
    for a in range(1, 4):
        send(yb.at[y], yb.at[y], s_yb + a, y_at(a))
    s_pb = new(1)
    send(yb.at[y], pb, s_pb, partner)

    for i in range(2):
        back[1].forward(i)
    back_first(0)
    out_last(0)
    for i in range(2):
        back[0].forward(i)
    out_last(1)
    got(orecv.at[0], s_of[0])
    o_out[rows((1 - k) * 96, 96)] = (orecv[0] + bd_in[...]).astype(BF16)
    for a in range(1, 4):
        got(yb.at[lax.rem(y + 4 - a, 4)], s_yb + a)
    got(pb, s_pb)
    bu_out[0:5] = yb[2 * k][0:5]
    bu_out[5:10] = yb[2 * k + 1][0:5]
    bd_out[0:10] = jnp.where(k == hh, yb[y][5:15], pb[5:15])
    got(orecv.at[1], s_of[1])
    gi_out[rows((1 - k) * 96, 96)] = orecv[1].astype(BF16)
    back[1].finish()
    back[0].finish()

    for copy, when in sent:
        if when is None:
            copy.wait_send()
        else:

            @pl.when(when)
            def _(copy=copy):
                copy.wait_send()

    assert used[0] <= N_SEMS, used[0]


def per_device(tokens, up_weight, up_bias, down_weight, down_bias, out_grad):
    token_rows = tokens.shape[0]
    scale = 1.0 / math.sqrt(token_rows * lax.axis_size("col") * lax.axis_size("depth"))
    vmem = pl.BlockSpec(memory_space=pltpu.VMEM)
    hbm = pl.BlockSpec(memory_space=pl.ANY)
    scratch = [
        ((2, 96, 320), BF16),
        ((2, 96, 640), BF16),
        ((4, 80, 640), BF16),
        ((8, 1280), F32),
        ((8, 1280), F32),
        ((2, 2, 768, 640), BF16),
        ((2, 2, 2, 320, 640), BF16),
        ((2, 2, 2, 320, 768), BF16),
        ((2, 384, 640), F32),
        ((2, 384, 640), F32),
        ((384, 640), F32),
        ((384, 640), F32),
        ((768, 640), BF16),
        ((768, 640), BF16),
        ((2, 2, 768, 640), BF16),
        ((2, 2, 192, 640), BF16),
        ((2, 2, 2, 192, 640), BF16),
        ((2, 2, 192, 640), BF16),
        ((2, 4, 96, 640), BF16),
        ((2, 96, 320), F32),
        ((2, 96, 320), F32),
        ((2, 2, 2, 320, 640), BF16),
        ((2, 2, 2, 80, 640), BF16),
        ((2, 2, 2, 2, 80, 640), BF16),
        ((2, 2, 2, 80, 640), F32),
        ((2, 2, 80, 640), BF16),
        ((2, 2, 80, 640), BF16),
        ((2, 2, 80, 640), BF16),
        ((16, 128), F32),
        ((8, 16, 128), F32),
        ((4, 16, 128), F32),
        ((16, 128), F32),
    ]
    out = pl.pallas_call(
        lambda *refs: kernel(scale, *refs),
        name="mlp_block",
        out_shape=[
            jax.ShapeDtypeStruct((192, 320), BF16),
            jax.ShapeDtypeStruct((192, 320), BF16),
            jax.ShapeDtypeStruct((2, 320, 1280), BF16),
            jax.ShapeDtypeStruct((320, 2560), BF16),
            jax.ShapeDtypeStruct((16, 128), F32),
            jax.ShapeDtypeStruct((16, 128), F32),
        ],
        in_specs=[vmem, hbm, vmem, hbm, vmem, vmem],
        out_specs=[vmem] * 6,
        scratch_shapes=[pltpu.VMEM(*s) for s in scratch] + [pltpu.SemaphoreType.DMA((N_SEMS,))],
        compiler_params=pltpu.CompilerParams(
            collective_id=0, has_side_effects=True, vmem_limit_bytes=56 << 20
        ),
        cost_estimate=pl.CostEstimate(
            flops=6 * 2 * 768 * 1280 * 640, bytes_accessed=12 << 20, transcendentals=384 * 640
        ),
    )(
        tokens,
        up_weight.reshape(2, 320, 1280),
        up_bias.reshape(1, 1280),
        down_weight.T,
        down_bias.reshape(1, 320),
        out_grad,
    )
    layer_out, grad_in, grad_up, grad_down, bu, bd = out
    row = lax.axis_index("row")
    grad_up_bias = bu[:10].reshape(1280).astype(BF16)
    start = lax.rem(row // 2, 2) * 640 + lax.rem(row, 2) * 320
    grad_down_bias = lax.dynamic_slice(bd[:10].reshape(1280), (start,), (320,)).astype(BF16)
    grad_up = grad_up.reshape(640, 1280)
    return (layer_out, grad_in, grad_up, grad_up_bias, grad_down.T, grad_down_bias)


def solution(mesh):
    return jax.shard_map(
        per_device,
        mesh=mesh,
        in_specs=(
            P(("col", "depth"), "row"),
            P("col", "row"),
            P("row"),
            P("col", "row"),
            P("row"),
            P(("col", "depth"), "row"),
        ),
        out_specs=(
            P(("col", "depth"), "row"),
            P(("col", "depth"), "row"),
            P("col", "row"),
            P("row"),
            P("col", "row"),
            P("row"),
        ),
        check_vma=False,
    )
```

```python
import math

import jax
import jax.numpy as jnp
from jax import lax
from jax.experimental import pallas as pl
from jax.experimental.pallas import tpu as pltpu
from jax.sharding import PartitionSpec as P

GELU_C = math.sqrt(2.0 / math.pi)
MESH = pl.DeviceIdType.MESH
F32 = jnp.float32
BF16 = jnp.bfloat16
N_SEMS = 320


def gelu_parts(v):
    t = jnp.tanh(GELU_C * (v + 0.044715 * v * v * v))
    value = 0.5 * v * (1.0 + t)
    slope = 0.5 * (1.0 + t) + 0.5 * v * (1.0 - t * t) * GELU_C * (1.0 + 3.0 * 0.044715 * v * v)
    return value, slope


def nn(a, b):
    return lax.dot_general(a, b, (((1,), (0,)), ((), ())), preferred_element_type=F32)


def nt(a, b):
    return lax.dot_general(a, b, (((1,), (1,)), ((), ())), preferred_element_type=F32)


def rows(start, size, tile=16):
    return pl.ds(pl.multiple_of(start, tile), size)


def kernel(
    scale,
    tok, wu_in, bu_in, wd_in, bd_in, grad,
    o_out, gi_out, gu_out, gd_out, bu_out, bd_out,
    xo, xr, bu, bd, piece, wq, bb, bbr,
    full, wts, full_t,
    hps, hpr, hpo, slope, act, dhid,
    part, ra, rb, xsum, zr, osend, orecv,
    gpart, ga, gb, gsum, gs, gz, gfin,
    bt, br, yb, pb,
    sems,
):
    row, y, dep = lax.axis_index("row"), lax.axis_index("col"), lax.axis_index("depth")
    h, k = row // 2, lax.rem(row, 2)
    zl, x = dep // 4, lax.rem(dep, 4)
    hh = h // 2
    hi = lax.rem(h, 2)

    def at(h_, k_, y_, plane):
        return (h_ * 2 + k_, y_, plane * 4 + x)

    def is_me(h_, k_, y_, plane):
        return (h_ == h) & (k_ == k) & (y_ == y) & (plane == zl)

    def z_at(a):
        return (lax.rem(h + a, 4) * 2 + k, y, dep)

    def dep_at(a, b):
        return (row, y, lax.rem(zl + b, 2) * 4 + lax.rem(x + a, 4))

    def y_at(a):
        return (row, lax.rem(y + a, 4), dep)

    partner = (h * 2 + 1 - k, y, dep)
    zpeer = dep_at(0, 1)

    local = [
        pltpu.make_async_copy(src, dst, sems.at[n])
        for n, (src, dst) in enumerate(
            (
                (bu_in, bu),
                (tok.at[rows(k * 96, 96)], xo.at[0]),
                (grad.at[rows(k * 96, 96)], xo.at[1]),
                (bd_in, bd),
            )
        )
    ]
    for copy in local:
        copy.start()

    bar = pltpu.get_barrier_semaphore()
    fixed = [partner, z_at(1), z_at(3)] + [y_at(a) for a in (1, 2, 3)]
    fixed += [dep_at(a, b) for a in range(4) for b in range(2) if (a, b) != (0, 0)]
    for target in fixed:
        pl.semaphore_signal(bar, inc=1, device_id=target, device_id_type=MESH)
    count = len(fixed)

    def greet(*place):
        other = jnp.logical_not(is_me(*place))

        @pl.when(other)
        def _():
            pl.semaphore_signal(bar, inc=1, device_id=at(*place), device_id_type=MESH)

        return other.astype(jnp.int32)

    for a in range(4):
        count = count + greet(a, hh, y, zl)
        count = count + greet(y, hh, a, k)
    for a in range(2):
        for b in range(2):
            count = count + greet(2 * k + a, b, y, zl)
            count = count + greet(2 * k + a, zl, h, b)
            count = count + greet(h, y // 2, 2 * k + a, b)
    pl.semaphore_wait(bar, count)

    used = [len(local)]
    sent = []

    def new(n=1):
        first = used[0]
        used[0] += n
        return first

    def send(src, dst, rsem, target):
        copy = pltpu.make_async_remote_copy(
            src_ref=src, dst_ref=dst, send_sem=sems.at[new()], recv_sem=sems.at[rsem],
            device_id=target, device_id_type=MESH,
        )
        copy.start()
        sent.append((copy, None))

    def send_if(only, src, dst, rsem, *place):
        mine = is_me(*place)
        away = jnp.logical_not(mine) & only
        copy = pltpu.make_async_remote_copy(
            src_ref=src, dst_ref=dst, send_sem=sems.at[new()], recv_sem=sems.at[rsem],
            device_id=at(*place), device_id_type=MESH,
        )

        @pl.when(away)
        def _():
            copy.start()

        @pl.when(mine & only)
        def _():
            pltpu.make_async_copy(src, dst, sems.at[rsem]).start()

        sent.append((copy, away))

    def got(dst, rsem):
        pltpu.make_async_copy(dst, dst, sems.at[rsem]).wait()

    def got_if(only, dst, rsem):
        @pl.when(only)
        def _():
            got(dst, rsem)

    def token_view(buf):
        return lambda i, q: buf.at[i, rows(lax.rem(q, 4) * 192, 192)]

    def half_view(buf, i):
        return lambda kk, q: buf.at[i, rows(lax.rem(q, 4) * 192 + kk * 96, 96)]

    def chunk_view(buf):
        return lambda i, q: buf.at[i, :, rows(lax.rem(q, 4) * 80, 80)]

    def chunk_half_view(buf, i):
        return lambda kk, q: buf.at[i, kk, rows(lax.rem(q, 4) * 80, 80)]

    def ring(axis):
        if axis == "y":
            return y, y_at(1), y_at(3)
        return x, dep_at(1, 0), dep_at(3, 0)

    class Gather:
        def __init__(self, view, axis):
            self.p, self.right, self.left = ring(axis)
            self.view = view
            self.s_right, self.s_left, self.s_fwd = new(2), new(2), new(2)

        def first(self, i):
            mine = self.view(i, self.p)
            pair = [(self.s_right + i, self.right), (self.s_left + i, self.left)]
            for sem, target in pair if i == 0 else pair[::-1]:
                send(mine, mine, sem, target)

        def forward(self, i):
            if i == 0:
                block = self.view(0, self.p + 3)
                got(block, self.s_right)
                send(block, block, self.s_fwd, self.right)
            else:
                block = self.view(1, self.p + 1)
                got(block, self.s_left + 1)
                send(block, block, self.s_fwd + 1, self.left)

        def finish(self):
            got(self.view(1, self.p + 3), self.s_right + 1)
            got(self.view(0, self.p + 1), self.s_left)
            got(self.view(0, self.p + 2), self.s_fwd)
            got(self.view(1, self.p + 2), self.s_fwd + 1)

    class Reduce:
        def __init__(self, view, first, second, axis):
            self.p, self.right, self.left = ring(axis)
            self.view = view
            self.first, self.second = first, second
            self.s1, self.s2 = new(2), new(4)

        def far(self):
            send(self.view(0, self.p + 2), self.first.at[0], self.s1, self.right)
            send(self.view(1, self.p + 2), self.first.at[1], self.s1 + 1, self.left)

        def near(self):
            send(self.view(1, self.p + 1), self.second.at[0, 1], self.s2 + 1, self.right)
            send(self.view(0, self.p + 3), self.second.at[1, 0], self.s2 + 2, self.left)

        def middle(self):
            for i, q, target in ((0, self.p + 1, self.right), (1, self.p + 3, self.left)):
                got(self.first.at[i], self.s1 + i)
                block = self.view(i, q)
                block[...] = (block[...].astype(F32) + self.first[i].astype(F32)).astype(BF16)
                send(block, self.second.at[i, i], self.s2 + 3 * i, target)

        def total(self, i):
            got(self.second.at[0, i], self.s2 + i)
            got(self.second.at[1, i], self.s2 + 2 + i)
            return (
                self.view(i, self.p)[...].astype(F32)
                + self.second[0, i].astype(F32)
                + self.second[1, i].astype(F32)
            )

    def pair_lanes(own, other):
        first = jnp.where(k == 0, own, other).astype(F32)
        second = jnp.where(k == 0, other, own).astype(F32)
        return jnp.concatenate([first, second], axis=1).astype(BF16)

    def split_lanes(both):
        low, high = both[:, :320], both[:, 320:]
        return jnp.where(k == 0, low, high), jnp.where(k == 0, high, low)

    s_x = new(2)
    for n, src in enumerate((tok, grad)):
        send(src.at[rows((1 - k) * 96, 96)], xr.at[n], s_x + n, partner)
    quarter = rows(x * 80, 80)
    always = k >= 0

    def lanes(n):
        return pl.ds(pl.multiple_of(n * 640, 128), 640)

    s_w = [new(2), new(4)]
    for j in range(2):
        send_if(
            always,
            wu_in.at[:, quarter, pl.ds(j * 640, 640)],
            wts.at[0, lax.rem(y, 2), :, quarter],
            s_w[0] + lax.rem(y, 2), h, y // 2, 2 * k + j, zl,
        )
    s_wq = new(4)
    for a in range(4):
        y_to = lax.rem(y + a, 4)
        send_if(always, wd_in.at[quarter, lanes(y_to)], wq.at[y], s_wq + a, h, k, y_to, zl)
    for copy in local:
        copy.wait()
    bb[...] = jnp.broadcast_to(bu[...].reshape(1, 1280), bb.shape)
    bd_row = bd[...].reshape(1, 320)
    s_bb = new(1)
    send(bb, bbr, s_bb, partner)

    s_piece = [new(4), new(4)]
    to_right = [h == lax.rem(2 * k + i + 1, 4) for i in range(2)]
    to_left = [h == lax.rem(2 * k + i + 3, 4) for i in range(2)]

    def part_of(n, i, kk):
        return full.at[n, i, rows(y * 192 + kk * 96, 96)]

    def send_piece(n):
        got(xr.at[n], s_x + n)
        piece[n] = pair_lanes(xo[n], xr[n])
        dst = part_of(n, hi, k)
        sem = s_piece[n] + hi * 2 + k
        for a in (1, 3):
            send_if(always, piece.at[n], dst, sem, lax.rem(h + a, 4), hh, y, zl)
        send_if(always, piece.at[n], dst, sem, h, hh, y, zl)

    def pass_piece(n):
        for i in range(2):
            for kk, only, a in ((0, to_right[i], 1), (1, to_left[i], 3)):
                sem = s_piece[n] + i * 2 + kk
                block = part_of(n, i, kk)
                got_if(only, block, sem)
                send_if(only, block, block, sem, lax.rem(h + a, 4), k, y, zl)

    def got_piece(n, i, kk):
        only = (to_right, to_left)[kk][i]
        got_if(jnp.logical_not(only), part_of(n, i, kk), s_piece[n] + i * 2 + kk)

    wag = [Gather(chunk_view(wts.at[n]), "x") for n in range(2)]
    tag = [[Gather(half_view(full.at[n], i), "y") for i in range(2)] for n in range(2)]

    def over_y(n, i, kk):
        got_piece(n, i, kk)
        tag[n][i].first(kk)

    send_piece(0)
    for i in range(2):
        got(wts.at[0, i, :, quarter], s_w[0] + i)
        wag[0].first(i)
    pass_piece(0)
    for a in range(4):
        origin = lax.rem(y + 4 - a, 4)
        got(wq.at[origin], s_wq + a)
        send_if(
            always, wq.at[origin], wts.at[1, hi, k, quarter], s_w[1] + hi * 2 + k, origin, hh, y, zl
        )
    for i in range(2):
        for kk in range(2):
            over_y(0, i, kk)
    send_piece(1)
    for i in range(2):
        wag[0].forward(i)
    for i in range(2):
        for kk in range(2):
            tag[0][i].forward(kk)
    for i in range(2):
        for kk in range(2):
            got(wts.at[1, i, kk, quarter], s_w[1] + i * 2 + kk)
        wag[1].first(i)
    pass_piece(1)
    over_y(1, 0, 0)
    over_y(1, 0, 1)
    over_y(1, 1, 0)

    half = 384
    own_rows = rows(k * half, half)
    other_rows = rows((1 - k) * half, half)

    def weight(n, i):
        return wts[n, i].reshape(640, 640)

    def hidden(n, block):
        return nn(full[n, 0, block], weight(n, 0)) + nn(full[n, 1, block], weight(n, 1))

    def transpose(n, i):
        full_t[n, i] = full[n, i].T.reshape(2, 320, 768)

    s_hp, s_act = [new(1), new(1)], [new(1), new(1)]
    tag[0][0].finish()
    tag[0][1].finish()
    wag[0].finish()
    hps[0] = hidden(0, other_rows)
    send(hps.at[0], hpr.at[0], s_hp[0], partner)
    hpo[...] = hidden(0, own_rows)
    for kk in range(2):
        tag[1][0].forward(kk)
    over_y(1, 1, 1)
    for i in range(2):
        wag[1].forward(i)
    got(bbr, s_bb)
    low = jnp.where(k == y // 2, bb[0:1], bbr[0:1])
    bias = jnp.where(lax.rem(y, 2) == 0, low[:, :640], low[:, 640:])
    got(hpr.at[0], s_hp[0])
    value, slope_now = gelu_parts(hpo[...] + hpr[0] + bias)
    slope[...] = slope_now
    act[own_rows] = value.astype(BF16)
    send(act.at[own_rows], act.at[own_rows], s_act[0], partner)
    for i in range(2):
        transpose(0, i)
    got(act.at[other_rows], s_act[0])

    ored = [Reduce(token_view(part.at[n]), ra.at[n], rb.at[n], "y") for n in range(2)]
    gred = [
        [Reduce(chunk_half_view(gpart.at[n], i), ga.at[n, i], gb.at[n, i], "x") for i in range(2)]
        for n in range(2)
    ]

    def out_block(n, q):
        block = rows(lax.rem(q, 4) * 192, 192)
        left = act if n == 0 else dhid
        for i in range(2):
            part[n, i, block] = nt(left[block], weight(1 - n, i)).astype(BF16)

    def grad_block(n, i, q):
        block = rows(lax.rem(q, 4) * 80, 80)
        right = dhid if n == 0 else act
        left = full_t[n, i, :, block].reshape(160, 768)
        gpart[n, i, :, block] = (nn(left, right[...]) * scale).astype(BF16).reshape(2, 80, 640)

    def grad_start(n, i):
        grad_block(n, i, x + 2)
        gred[n][i].far()
        grad_block(n, i, x + 1)
        grad_block(n, i, x + 3)
        gred[n][i].near()

    def grad_middle(n, i):
        grad_block(n, i, x)
        gred[n][i].middle()

    s_oz = [new(4), new(4)]

    def out_z(n):
        for i in range(2):
            xsum[n, i] = ored[n].total(i).astype(BF16)
            for kk in range(2):
                send_if(
                    always, xsum.at[n, i, pl.ds(kk * 96, 96)], zr.at[n, h], s_oz[n] + h,
                    2 * k + i, kk, y, zl,
                )

    s_gz, s_gr = [new(2), new(2)], [new(4), new(4)]

    def grad_zl(n, i):
        for kk in range(2):
            gsum[n, i, kk] = gred[n][i].total(kk)
        gs[n, i] = gsum[n, i, 1 - zl].astype(BF16)
        send(gs.at[n, i], gz.at[n, i], s_gz[n] + i, zpeer)

    def grad_home(n, i):
        got(gz.at[n, i], s_gz[n] + i)
        gfin[n, i] = (gsum[n, i, zl] + gz[n, i].astype(F32)).astype(BF16)
        for p in range(2):
            plane = lax.rem(zl + 1 - p, 2)
            if n == 0:
                send_if(
                    always, gfin.at[0, i], gu_out.at[zl, quarter, lanes(lax.rem(y, 2))],
                    s_gr[0] + 2 * (1 - p) + lax.rem(y, 2), h, y // 2, 2 * k + i, plane,
                )
            else:
                send_if(
                    always, gfin.at[1, i], gd_out.at[quarter, lanes(y)],
                    s_gr[1] + y, 2 * k + i, zl, h, plane,
                )

    back = [
        Gather(lambda i, q: gu_out.at[:, rows(lax.rem(q, 4) * 80, 80), pl.ds(i * 640, 640)], "x"),
        Gather(lambda i, q: gd_out.at[rows(lax.rem(q, 4) * 80, 80), pl.ds(i * 1280, 1280)], "x"),
    ]

    def back_first(n):
        for i in range(2):
            if n == 0:
                got(gu_out.at[zl, quarter, pl.ds(i * 640, 640)], s_gr[0] + i)
                got(gu_out.at[1 - zl, quarter, pl.ds(i * 640, 640)], s_gr[0] + 2 + i)
            else:
                for j in range(2):
                    got(gd_out.at[quarter, pl.ds((2 * i + j) * 640, 640)], s_gr[1] + 2 * i + j)
            back[n].first(i)

    s_of = [new(1), new(1)]

    def out_last(n):
        total = jnp.zeros((96, 640), F32)
        for a in range(4):
            got(zr.at[n, a], s_oz[n] + a)
            total = total + zr[n, a].astype(F32)
        mine, theirs = split_lanes(total)
        osend[n] = theirs
        send(osend.at[n], orecv.at[n], s_of[n], partner)
        if n == 0:
            o_out[rows(k * 96, 96)] = (mine + bd_row).astype(BF16)
        else:
            gi_out[rows(k * 96, 96)] = mine.astype(BF16)

    tag[1][0].finish()
    transpose(1, 0)
    grad_start(1, 0)
    for kk in range(2):
        tag[1][1].forward(kk)
    wag[1].finish()
    out_block(0, y + 2)
    ored[0].far()
    grad_middle(1, 0)
    out_block(0, y + 1)
    out_block(0, y + 3)
    ored[0].near()
    tag[1][1].finish()
    hps[1] = hidden(1, other_rows)
    send(hps.at[1], hpr.at[1], s_hp[1], partner)
    transpose(1, 1)
    grad_start(1, 1)
    d_own = hidden(1, own_rows)
    got(hpr.at[1], s_hp[1])
    dhid[own_rows] = ((d_own + hpr[1]) * slope[...]).astype(BF16)
    send(dhid.at[own_rows], dhid.at[own_rows], s_act[1], partner)
    ored[0].middle()
    grad_zl(1, 0)
    grad_middle(1, 1)
    got(dhid.at[other_rows], s_act[1])
    grad_start(0, 0)
    out_block(1, y + 2)
    ored[1].far()
    grad_home(1, 0)
    grad_start(0, 1)
    grad_zl(1, 1)
    out_block(1, y + 1)
    out_block(1, y + 3)
    ored[1].near()
    grad_middle(0, 0)
    out_block(0, y)
    grad_home(1, 1)
    grad_middle(0, 1)
    ones = jnp.ones((16, 768), BF16)
    terms = [nn(ones, dhid[...]), nn(ones, full[1, 0]), nn(ones, full[1, 1])]
    bt[...] = jnp.zeros_like(bt)
    for n in range(15):
        term = terms[n // 5][0:1, (n % 5) * 128 : (n % 5 + 1) * 128] * scale
        bt[n : n + 1] = term.astype(BF16).astype(F32)
    br[dep] = bt[...]
    s_bt = new(8)
    for a in range(4):
        for b in range(2):
            if (a, b) != (0, 0):
                send(bt, br.at[dep], s_bt + a * 2 + b, dep_at(a, b))
    grad_zl(0, 0)
    ored[1].middle()
    grad_zl(0, 1)
    out_block(1, y)
    back_first(1)
    grad_home(0, 0)
    grad_home(0, 1)
    out_z(0)
    out_z(1)
    for i in range(2):
        back[1].forward(i)

    back_first(0)
    for a in range(4):
        for b in range(2):
            if (a, b) != (0, 0):
                from_dep = lax.rem(zl + b, 2) * 4 + lax.rem(x + 4 - a, 4)
                got(br.at[from_dep], s_bt + a * 2 + b)
    total = br[0]
    for n in range(1, 8):
        total = total + br[n]
    yb[y] = total
    s_yb = new(4)
    for a in range(1, 4):
        send(yb.at[y], yb.at[y], s_yb + a, y_at(a))
    s_pb = new(1)
    send(yb.at[y], pb, s_pb, partner)

    out_last(0)
    for i in range(2):
        back[0].forward(i)
    out_last(1)
    got(orecv.at[0], s_of[0])
    o_out[rows((1 - k) * 96, 96)] = (orecv[0] + bd_row).astype(BF16)
    for a in range(1, 4):
        got(yb.at[lax.rem(y + 4 - a, 4)], s_yb + a)
    got(pb, s_pb)
    wide = [yb[2 * k + j][n : n + 1] for j in range(2) for n in range(5)]
    bu_out[...] = jnp.concatenate(wide, axis=1).astype(BF16).reshape(1280)
    from_tile = jnp.where(k == hh, yb[y], pb[...])
    wide = jnp.concatenate([from_tile[n : n + 1] for n in range(5, 15)], axis=1)
    wide = jnp.where(hi == 0, wide[:, :640], wide[:, 640:])
    bd_out[...] = jnp.where(k == 0, wide[:, :320], wide[:, 320:]).astype(BF16).reshape(320)
    got(orecv.at[1], s_of[1])
    gi_out[rows((1 - k) * 96, 96)] = orecv[1].astype(BF16)
    back[1].finish()
    back[0].finish()

    for copy, when in sent:
        if when is None:
            copy.wait_send()
        else:

            @pl.when(when)
            def _(copy=copy):
                copy.wait_send()

    assert used[0] <= N_SEMS, used[0]


def write_back(*refs):
    sems = refs[-1]
    copies = [
        pltpu.make_async_copy(refs[n], refs[6 + n], sems.at[n]) for n in range(6)
    ]
    for copy in copies:
        copy.start()
    for copy in copies:
        copy.wait()


def per_device(tokens, up_weight, up_bias, down_weight, down_bias, out_grad):
    token_rows = tokens.shape[0]
    scale = 1.0 / math.sqrt(token_rows * lax.axis_size("col") * lax.axis_size("depth"))
    vmem = pl.BlockSpec(memory_space=pltpu.VMEM)
    hbm = pl.BlockSpec(memory_space=pl.ANY)
    scratch = [
        ((2, 96, 320), BF16),
        ((2, 96, 320), BF16),
        ((1280,), F32),
        ((320,), F32),
        ((2, 96, 640), BF16),
        ((4, 80, 640), BF16),
        ((8, 1280), F32),
        ((8, 1280), F32),
        ((2, 2, 768, 640), BF16),
        ((2, 2, 2, 320, 640), BF16),
        ((2, 2, 2, 320, 768), BF16),
        ((2, 384, 640), F32),
        ((2, 384, 640), F32),
        ((384, 640), F32),
        ((384, 640), F32),
        ((768, 640), BF16),
        ((768, 640), BF16),
        ((2, 2, 768, 640), BF16),
        ((2, 2, 192, 640), BF16),
        ((2, 2, 2, 192, 640), BF16),
        ((2, 2, 192, 640), BF16),
        ((2, 4, 96, 640), BF16),
        ((2, 96, 320), F32),
        ((2, 96, 320), F32),
        ((2, 2, 2, 320, 640), BF16),
        ((2, 2, 2, 80, 640), BF16),
        ((2, 2, 2, 2, 80, 640), BF16),
        ((2, 2, 2, 80, 640), F32),
        ((2, 2, 80, 640), BF16),
        ((2, 2, 80, 640), BF16),
        ((2, 2, 80, 640), BF16),
        ((16, 128), F32),
        ((8, 16, 128), F32),
        ((4, 16, 128), F32),
        ((16, 128), F32),
    ]
    out = pl.pallas_call(
        lambda *refs: kernel(scale, *refs),
        name="mlp_block",
        out_shape=[
            pltpu.VMEM((192, 320), BF16),
            pltpu.VMEM((192, 320), BF16),
            pltpu.VMEM((2, 320, 1280), BF16),
            pltpu.VMEM((320, 2560), BF16),
            pltpu.VMEM((1280,), BF16),
            pltpu.VMEM((320,), BF16),
        ],
        in_specs=[hbm] * 6,
        out_specs=[vmem] * 6,
        scratch_shapes=[pltpu.VMEM(*s) for s in scratch] + [pltpu.SemaphoreType.DMA((N_SEMS,))],
        compiler_params=pltpu.CompilerParams(
            collective_id=0, has_side_effects=True, vmem_limit_bytes=44 << 20
        ),
        cost_estimate=pl.CostEstimate(
            flops=6 * 2 * 768 * 1280 * 640, bytes_accessed=12 << 20, transcendentals=384 * 640
        ),
    )(
        *[
            pltpu.with_memory_space_constraint(a, pltpu.HBM)
            for a in (
                tokens, up_weight.reshape(2, 320, 1280), up_bias, down_weight.T, down_bias, out_grad
            )
        ]
    )
    layer_out, grad_in, grad_up, grad_down, bu, bd = pl.pallas_call(
        write_back,
        name="write_back",
        out_shape=[jax.ShapeDtypeStruct(a.shape, a.dtype) for a in out],
        in_specs=[vmem] * 6,
        out_specs=[hbm] * 6,
        scratch_shapes=[pltpu.SemaphoreType.DMA((6,))],
        compiler_params=pltpu.CompilerParams(vmem_limit_bytes=1 << 20),
        cost_estimate=pl.CostEstimate(flops=0, bytes_accessed=8 << 20, transcendentals=0),
    )(*[pltpu.with_memory_space_constraint(a, pltpu.VMEM) for a in out])
    return (layer_out, grad_in, grad_up.reshape(640, 1280), bu, grad_down.T, bd)


def solution(mesh):
    return jax.shard_map(
        per_device,
        mesh=mesh,
        in_specs=(
            P(("col", "depth"), "row"),
            P("col", "row"),
            P("row"),
            P("col", "row"),
            P("row"),
            P(("col", "depth"), "row"),
        ),
        out_specs=(
            P(("col", "depth"), "row"),
            P(("col", "depth"), "row"),
            P("col", "row"),
            P("row"),
            P("col", "row"),
            P("row"),
        ),
        check_vma=False,
    )
```

```python
import math

import jax
import jax.numpy as jnp
from jax import lax
from jax.experimental import pallas as pl
from jax.experimental.pallas import tpu as pltpu
from jax.sharding import PartitionSpec as P

GELU_C = math.sqrt(2.0 / math.pi)
MESH = pl.DeviceIdType.MESH
F32 = jnp.float32
BF16 = jnp.bfloat16
N_SEMS = 320


def gelu_parts(v):
    t = jnp.tanh(GELU_C * (v + 0.044715 * v * v * v))
    value = 0.5 * v * (1.0 + t)
    slope = 0.5 * (1.0 + t) + 0.5 * v * (1.0 - t * t) * GELU_C * (1.0 + 3.0 * 0.044715 * v * v)
    return value, slope


def nn(a, b):
    return lax.dot_general(a, b, (((1,), (0,)), ((), ())), preferred_element_type=F32)


def nt(a, b):
    return lax.dot_general(a, b, (((1,), (1,)), ((), ())), preferred_element_type=F32)


def rows(start, size, tile=16):
    return pl.ds(pl.multiple_of(start, tile), size)


def kernel(
    scale,
    tok, wu_in, bu_in, wd_in, bd_in, grad,
    o_out, gi_out, gu_out, gd_out, bu_out, bd_out,
    xo, xr, bu, bd, piece, wq, bb, bbr,
    full, wts, full_t,
    hps, hpr, hpo, slope, act, dhid,
    part, ra, rb, xsum, zr, osend, orecv,
    gpart, ga, gb, gsum, gs, gz, gfin,
    bt, br, yb, pb,
    sems,
):
    row, y, dep = lax.axis_index("row"), lax.axis_index("col"), lax.axis_index("depth")
    h, k = row // 2, lax.rem(row, 2)
    zl, x = dep // 4, lax.rem(dep, 4)
    hh = h // 2
    hi = lax.rem(h, 2)

    def at(h_, k_, y_, plane):
        return (h_ * 2 + k_, y_, plane * 4 + x)

    def is_me(h_, k_, y_, plane):
        return (h_ == h) & (k_ == k) & (y_ == y) & (plane == zl)

    def z_at(a):
        return (lax.rem(h + a, 4) * 2 + k, y, dep)

    def dep_at(a, b):
        return (row, y, lax.rem(zl + b, 2) * 4 + lax.rem(x + a, 4))

    def y_at(a):
        return (row, lax.rem(y + a, 4), dep)

    partner = (h * 2 + 1 - k, y, dep)
    zpeer = dep_at(0, 1)

    local = [
        pltpu.make_async_copy(src, dst, sems.at[n])
        for n, (src, dst) in enumerate(
            (
                (bu_in, bu),
                (tok.at[rows(k * 96, 96)], xo.at[0]),
                (grad.at[rows(k * 96, 96)], xo.at[1]),
                (bd_in, bd),
            )
        )
    ]
    for copy in local:
        copy.start()

    bar = pltpu.get_barrier_semaphore()
    fixed = [partner, z_at(1), z_at(3)] + [y_at(a) for a in (1, 2, 3)]
    fixed += [dep_at(a, b) for a in range(4) for b in range(2) if (a, b) != (0, 0)]
    for target in fixed:
        pl.semaphore_signal(bar, inc=1, device_id=target, device_id_type=MESH)
    count = len(fixed)

    def greet(*place):
        other = jnp.logical_not(is_me(*place))

        @pl.when(other)
        def _():
            pl.semaphore_signal(bar, inc=1, device_id=at(*place), device_id_type=MESH)

        return other.astype(jnp.int32)

    for a in range(4):
        count = count + greet(a, hh, y, zl)
        count = count + greet(y, hh, a, k)
    for a in range(2):
        for b in range(2):
            count = count + greet(2 * k + a, b, y, zl)
            count = count + greet(2 * k + a, zl, h, b)
            count = count + greet(h, y // 2, 2 * k + a, b)
    pl.semaphore_wait(bar, count)

    used = [len(local)]
    sent = []

    def new(n=1):
        first = used[0]
        used[0] += n
        return first

    def send(src, dst, rsem, target):
        copy = pltpu.make_async_remote_copy(
            src_ref=src, dst_ref=dst, send_sem=sems.at[new()], recv_sem=sems.at[rsem],
            device_id=target, device_id_type=MESH,
        )
        copy.start()
        sent.append((copy, None))

    def send_if(only, src, dst, rsem, *place):
        mine = is_me(*place)
        away = jnp.logical_not(mine) & only
        copy = pltpu.make_async_remote_copy(
            src_ref=src, dst_ref=dst, send_sem=sems.at[new()], recv_sem=sems.at[rsem],
            device_id=at(*place), device_id_type=MESH,
        )

        @pl.when(away)
        def _():
            copy.start()

        @pl.when(mine & only)
        def _():
            pltpu.make_async_copy(src, dst, sems.at[rsem]).start()

        sent.append((copy, away))

    def got(dst, rsem):
        pltpu.make_async_copy(dst, dst, sems.at[rsem]).wait()

    def got_if(only, dst, rsem):
        @pl.when(only)
        def _():
            got(dst, rsem)

    def token_view(buf):
        return lambda i, q: buf.at[i, rows(lax.rem(q, 4) * 192, 192)]

    def half_view(buf, i):
        return lambda kk, q: buf.at[i, rows(lax.rem(q, 4) * 192 + kk * 96, 96)]

    def chunk_view(buf):
        return lambda i, q: buf.at[i, :, rows(lax.rem(q, 4) * 80, 80)]

    def chunk_half_view(buf, i):
        return lambda kk, q: buf.at[i, kk, rows(lax.rem(q, 4) * 80, 80)]

    def ring(axis):
        if axis == "y":
            return y, y_at(1), y_at(3)
        return x, dep_at(1, 0), dep_at(3, 0)

    class Gather:
        def __init__(self, view, axis):
            self.p, self.right, self.left = ring(axis)
            self.view = view
            self.s_right, self.s_left, self.s_fwd = new(2), new(2), new(2)

        def first(self, i):
            mine = self.view(i, self.p)
            pair = [(self.s_right + i, self.right), (self.s_left + i, self.left)]
            for sem, target in pair if i == 0 else pair[::-1]:
                send(mine, mine, sem, target)

        def forward(self, i):
            if i == 0:
                block = self.view(0, self.p + 3)
                got(block, self.s_right)
                send(block, block, self.s_fwd, self.right)
            else:
                block = self.view(1, self.p + 1)
                got(block, self.s_left + 1)
                send(block, block, self.s_fwd + 1, self.left)

        def finish(self):
            got(self.view(1, self.p + 3), self.s_right + 1)
            got(self.view(0, self.p + 1), self.s_left)
            got(self.view(0, self.p + 2), self.s_fwd)
            got(self.view(1, self.p + 2), self.s_fwd + 1)

    class Reduce:
        def __init__(self, view, first, second, axis):
            self.p, self.right, self.left = ring(axis)
            self.view = view
            self.first, self.second = first, second
            self.s1, self.s2 = new(2), new(4)

        def far(self):
            send(self.view(0, self.p + 2), self.first.at[0], self.s1, self.right)
            send(self.view(1, self.p + 2), self.first.at[1], self.s1 + 1, self.left)

        def near(self):
            send(self.view(1, self.p + 1), self.second.at[0, 1], self.s2 + 1, self.right)
            send(self.view(0, self.p + 3), self.second.at[1, 0], self.s2 + 2, self.left)

        def middle(self):
            for i, q, target in ((0, self.p + 1, self.right), (1, self.p + 3, self.left)):
                got(self.first.at[i], self.s1 + i)
                block = self.view(i, q)
                block[...] = (block[...].astype(F32) + self.first[i].astype(F32)).astype(BF16)
                send(block, self.second.at[i, i], self.s2 + 3 * i, target)

        def total(self, i):
            got(self.second.at[0, i], self.s2 + i)
            got(self.second.at[1, i], self.s2 + 2 + i)
            return (
                self.view(i, self.p)[...].astype(F32)
                + self.second[0, i].astype(F32)
                + self.second[1, i].astype(F32)
            )

    def pair_lanes(own, other):
        first = jnp.where(k == 0, own, other).astype(F32)
        second = jnp.where(k == 0, other, own).astype(F32)
        return jnp.concatenate([first, second], axis=1).astype(BF16)

    def split_lanes(both):
        low, high = both[:, :320], both[:, 320:]
        return jnp.where(k == 0, low, high), jnp.where(k == 0, high, low)

    s_x = new(2)
    for n, src in enumerate((tok, grad)):
        send(src.at[rows((1 - k) * 96, 96)], xr.at[n], s_x + n, partner)
    quarter = rows(x * 80, 80)
    always = k >= 0
    near = jnp.where(hh == k, hi, 1 - hi)
    order = [near, 1 - near]

    def lanes(n):
        return pl.ds(pl.multiple_of(n * 640, 128), 640)

    s_w = [new(2), new(4)]
    for j in range(2):
        send_if(
            always,
            wu_in.at[:, quarter, pl.ds(j * 640, 640)],
            wts.at[0, lax.rem(y, 2), :, quarter],
            s_w[0] + lax.rem(y, 2), h, y // 2, 2 * k + j, zl,
        )
    s_wq = new(4)
    for a in range(4):
        y_to = lax.rem(y + a, 4)
        send_if(always, wd_in.at[quarter, lanes(y_to)], wq.at[y], s_wq + a, h, k, y_to, zl)
    for copy in local:
        copy.wait()
    bb[...] = jnp.broadcast_to(bu[...].reshape(1, 1280), bb.shape)
    bd_row = bd[...].reshape(1, 320)
    s_bb = new(1)
    send(bb, bbr, s_bb, partner)

    s_piece = [new(4), new(4)]

    def passes(i, kk):
        return h == lax.rem(2 * k + i + (1, 3)[kk], 4)

    def part_of(n, i, kk):
        return full.at[n, i, rows(y * 192 + kk * 96, 96)]

    def send_piece(n):
        got(xr.at[n], s_x + n)
        piece[n] = pair_lanes(xo[n], xr[n])
        dst = part_of(n, hi, k)
        sem = s_piece[n] + hi * 2 + k
        for a in (1, 3):
            send_if(always, piece.at[n], dst, sem, lax.rem(h + a, 4), hh, y, zl)
        send_if(always, piece.at[n], dst, sem, h, hh, y, zl)

    def pass_piece(n):
        for i in range(2):
            for kk, a in ((0, 1), (1, 3)):
                only = passes(i, kk)
                sem = s_piece[n] + i * 2 + kk
                block = part_of(n, i, kk)
                got_if(only, block, sem)
                send_if(only, block, block, sem, lax.rem(h + a, 4), k, y, zl)

    def got_piece(n, i, kk):
        got_if(jnp.logical_not(passes(i, kk)), part_of(n, i, kk), s_piece[n] + i * 2 + kk)

    wag = [Gather(chunk_view(wts.at[n]), "x") for n in range(2)]
    tag = [[Gather(half_view(full.at[n], i), "y") for i in order] for n in range(2)]

    def over_y(n, i, kk):
        got_piece(n, order[i], kk)
        tag[n][i].first(kk)

    send_piece(0)
    for i in range(2):
        got(wts.at[0, i, :, quarter], s_w[0] + i)
        wag[0].first(i)
    pass_piece(0)
    for kk in range(2):
        over_y(0, 0, kk)
    for a in range(4):
        origin = lax.rem(y + 4 - a, 4)
        got(wq.at[origin], s_wq + a)
        send_if(
            always, wq.at[origin], wts.at[1, hi, k, quarter], s_w[1] + hi * 2 + k, origin, hh, y, zl
        )
    for kk in range(2):
        over_y(0, 1, kk)
    send_piece(1)
    for i in range(2):
        wag[0].forward(i)
    for i in range(2):
        for kk in range(2):
            tag[0][i].forward(kk)
    for i in range(2):
        for kk in range(2):
            got(wts.at[1, i, kk, quarter], s_w[1] + i * 2 + kk)
        wag[1].first(i)
    pass_piece(1)
    over_y(1, 0, 0)
    over_y(1, 0, 1)
    over_y(1, 1, 0)

    half = 384
    own_rows = rows(k * half, half)
    other_rows = rows((1 - k) * half, half)

    def weight(n, i):
        return wts[n, i].reshape(640, 640)

    def hidden(n, block):
        return nn(full[n, 0, block], weight(n, 0)) + nn(full[n, 1, block], weight(n, 1))

    def transpose(n, i):
        full_t[n, i] = full[n, i].T.reshape(2, 320, 768)

    s_hp, s_act = [new(1), new(1)], [new(1), new(1)]
    tag[0][0].finish()
    tag[0][1].finish()
    wag[0].finish()
    hps[0] = hidden(0, other_rows)
    send(hps.at[0], hpr.at[0], s_hp[0], partner)
    hpo[...] = hidden(0, own_rows)
    for kk in range(2):
        tag[1][0].forward(kk)
    over_y(1, 1, 1)
    for i in range(2):
        wag[1].forward(i)
    got(bbr, s_bb)
    low = jnp.where(k == y // 2, bb[0:1], bbr[0:1])
    bias = jnp.where(lax.rem(y, 2) == 0, low[:, :640], low[:, 640:])
    got(hpr.at[0], s_hp[0])
    value, slope_now = gelu_parts(hpo[...] + hpr[0] + bias)
    slope[...] = slope_now
    act[own_rows] = value.astype(BF16)
    send(act.at[own_rows], act.at[own_rows], s_act[0], partner)
    for i in range(2):
        transpose(0, i)
    got(act.at[other_rows], s_act[0])

    ored = [Reduce(token_view(part.at[n]), ra.at[n], rb.at[n], "y") for n in range(2)]
    gred = [
        [Reduce(chunk_half_view(gpart.at[n], i), ga.at[n, j], gb.at[n, j], "x") for j, i in enumerate(order)]
        for n in range(2)
    ]

    def out_block(n, q):
        block = rows(lax.rem(q, 4) * 192, 192)
        left = act if n == 0 else dhid
        for i in range(2):
            part[n, i, block] = nt(left[block], weight(1 - n, i)).astype(BF16)

    def grad_block(n, j, q):
        i = order[j]
        block = rows(lax.rem(q, 4) * 80, 80)
        right = dhid if n == 0 else act
        left = full_t[n, i, :, block].reshape(160, 768)
        gpart[n, i, :, block] = (nn(left, right[...]) * scale).astype(BF16).reshape(2, 80, 640)

    def grad_start(n, i):
        grad_block(n, i, x + 2)
        gred[n][i].far()
        grad_block(n, i, x + 1)
        grad_block(n, i, x + 3)
        gred[n][i].near()

    def grad_middle(n, i):
        grad_block(n, i, x)
        gred[n][i].middle()

    s_oz = [new(4), new(4)]

    def out_z(n):
        for i in range(2):
            xsum[n, i] = ored[n].total(i).astype(BF16)
            for kk in range(2):
                send_if(
                    always, xsum.at[n, i, pl.ds(kk * 96, 96)], zr.at[n, h], s_oz[n] + h,
                    2 * k + i, kk, y, zl,
                )

    s_gz, s_gr = [new(2), new(2)], [new(4), new(4)]

    def grad_zl(n, i):
        for kk in range(2):
            gsum[n, i, kk] = gred[n][i].total(kk)
        gs[n, i] = gsum[n, i, 1 - zl].astype(BF16)
        send(gs.at[n, i], gz.at[n, i], s_gz[n] + i, zpeer)

    def grad_home(n, i):
        got(gz.at[n, i], s_gz[n] + i)
        gfin[n, i] = (gsum[n, i, zl] + gz[n, i].astype(F32)).astype(BF16)
        to = 2 * k + order[i]
        for p in range(2):
            plane = lax.rem(zl + 1 - p, 2)
            if n == 0:
                send_if(
                    always, gfin.at[0, i], gu_out.at[zl, quarter, lanes(lax.rem(y, 2))],
                    s_gr[0] + 2 * (1 - p) + lax.rem(y, 2), h, y // 2, to, plane,
                )
            else:
                send_if(
                    always, gfin.at[1, i], gd_out.at[quarter, lanes(y)],
                    s_gr[1] + y, to, zl, h, plane,
                )

    back = [
        Gather(lambda i, q: gu_out.at[:, rows(lax.rem(q, 4) * 80, 80), pl.ds(i * 640, 640)], "x"),
        Gather(lambda i, q: gd_out.at[rows(lax.rem(q, 4) * 80, 80), pl.ds(i * 1280, 1280)], "x"),
    ]

    def back_first(n):
        for i in range(2):
            if n == 0:
                got(gu_out.at[zl, quarter, pl.ds(i * 640, 640)], s_gr[0] + i)
                got(gu_out.at[1 - zl, quarter, pl.ds(i * 640, 640)], s_gr[0] + 2 + i)
            else:
                for j in range(2):
                    got(gd_out.at[quarter, pl.ds((2 * i + j) * 640, 640)], s_gr[1] + 2 * i + j)
            back[n].first(i)

    s_of = [new(1), new(1)]

    def out_last(n):
        total = jnp.zeros((96, 640), F32)
        for a in range(4):
            got(zr.at[n, a], s_oz[n] + a)
            total = total + zr[n, a].astype(F32)
        mine, theirs = split_lanes(total)
        osend[n] = theirs
        send(osend.at[n], orecv.at[n], s_of[n], partner)
        if n == 0:
            o_out[rows(k * 96, 96)] = (mine + bd_row).astype(BF16)
        else:
            gi_out[rows(k * 96, 96)] = mine.astype(BF16)

    tag[1][0].finish()
    transpose(1, order[0])
    grad_start(1, 0)
    for kk in range(2):
        tag[1][1].forward(kk)
    wag[1].finish()
    out_block(0, y + 2)
    ored[0].far()
    grad_middle(1, 0)
    out_block(0, y + 1)
    out_block(0, y + 3)
    ored[0].near()
    tag[1][1].finish()
    hps[1] = hidden(1, other_rows)
    send(hps.at[1], hpr.at[1], s_hp[1], partner)
    transpose(1, order[1])
    grad_start(1, 1)
    d_own = hidden(1, own_rows)
    got(hpr.at[1], s_hp[1])
    dhid[own_rows] = ((d_own + hpr[1]) * slope[...]).astype(BF16)
    send(dhid.at[own_rows], dhid.at[own_rows], s_act[1], partner)
    ored[0].middle()
    grad_zl(1, 0)
    grad_middle(1, 1)
    got(dhid.at[other_rows], s_act[1])
    grad_start(0, 0)
    out_block(1, y + 2)
    ored[1].far()
    grad_home(1, 0)
    grad_start(0, 1)
    grad_zl(1, 1)
    out_block(1, y + 1)
    out_block(1, y + 3)
    ored[1].near()
    grad_middle(0, 0)
    out_block(0, y)
    grad_home(1, 1)
    grad_middle(0, 1)
    ones = jnp.ones((16, 768), BF16)
    terms = [nn(ones, dhid[...]), nn(ones, full[1, 0]), nn(ones, full[1, 1])]
    bt[...] = jnp.zeros_like(bt)
    for n in range(15):
        term = terms[n // 5][0:1, (n % 5) * 128 : (n % 5 + 1) * 128] * scale
        bt[n : n + 1] = term.astype(BF16).astype(F32)
    br[dep] = bt[...]
    s_bt = new(8)
    for a in range(4):
        for b in range(2):
            if (a, b) != (0, 0):
                send(bt, br.at[dep], s_bt + a * 2 + b, dep_at(a, b))
    grad_zl(0, 0)
    ored[1].middle()
    grad_zl(0, 1)
    out_block(1, y)
    back_first(1)
    grad_home(0, 0)
    grad_home(0, 1)
    out_z(0)
    out_z(1)
    for i in range(2):
        back[1].forward(i)

    back_first(0)
    for a in range(4):
        for b in range(2):
            if (a, b) != (0, 0):
                from_dep = lax.rem(zl + b, 2) * 4 + lax.rem(x + 4 - a, 4)
                got(br.at[from_dep], s_bt + a * 2 + b)
    total = br[0]
    for n in range(1, 8):
        total = total + br[n]
    yb[y] = total
    s_yb = new(4)
    for a in range(1, 4):
        send(yb.at[y], yb.at[y], s_yb + a, y_at(a))
    s_pb = new(1)
    send(yb.at[y], pb, s_pb, partner)

    out_last(0)
    for i in range(2):
        back[0].forward(i)
    out_last(1)
    got(orecv.at[0], s_of[0])
    o_out[rows((1 - k) * 96, 96)] = (orecv[0] + bd_row).astype(BF16)
    for a in range(1, 4):
        got(yb.at[lax.rem(y + 4 - a, 4)], s_yb + a)
    got(pb, s_pb)
    wide = [yb[2 * k + j][n : n + 1] for j in range(2) for n in range(5)]
    bu_out[...] = jnp.concatenate(wide, axis=1).astype(BF16).reshape(1280)
    from_tile = jnp.where(k == hh, yb[y], pb[...])
    wide = jnp.concatenate([from_tile[n : n + 1] for n in range(5, 15)], axis=1)
    wide = jnp.where(hi == 0, wide[:, :640], wide[:, 640:])
    bd_out[...] = jnp.where(k == 0, wide[:, :320], wide[:, 320:]).astype(BF16).reshape(320)
    got(orecv.at[1], s_of[1])
    gi_out[rows((1 - k) * 96, 96)] = orecv[1].astype(BF16)
    back[1].finish()
    back[0].finish()

    for copy, when in sent:
        if when is None:
            copy.wait_send()
        else:

            @pl.when(when)
            def _(copy=copy):
                copy.wait_send()

    assert used[0] <= N_SEMS, used[0]


def write_back(*refs):
    sems = refs[-1]
    copies = [
        pltpu.make_async_copy(refs[n], refs[6 + n], sems.at[n]) for n in range(6)
    ]
    for copy in copies:
        copy.start()
    for copy in copies:
        copy.wait()


def per_device(tokens, up_weight, up_bias, down_weight, down_bias, out_grad):
    token_rows = tokens.shape[0]
    scale = 1.0 / math.sqrt(token_rows * lax.axis_size("col") * lax.axis_size("depth"))
    vmem = pl.BlockSpec(memory_space=pltpu.VMEM)
    hbm = pl.BlockSpec(memory_space=pl.ANY)
    scratch = [
        ((2, 96, 320), BF16),
        ((2, 96, 320), BF16),
        ((1280,), F32),
        ((320,), F32),
        ((2, 96, 640), BF16),
        ((4, 80, 640), BF16),
        ((8, 1280), F32),
        ((8, 1280), F32),
        ((2, 2, 768, 640), BF16),
        ((2, 2, 2, 320, 640), BF16),
        ((2, 2, 2, 320, 768), BF16),
        ((2, 384, 640), F32),
        ((2, 384, 640), F32),
        ((384, 640), F32),
        ((384, 640), F32),
        ((768, 640), BF16),
        ((768, 640), BF16),
        ((2, 2, 768, 640), BF16),
        ((2, 2, 192, 640), BF16),
        ((2, 2, 2, 192, 640), BF16),
        ((2, 2, 192, 640), BF16),
        ((2, 4, 96, 640), BF16),
        ((2, 96, 320), F32),
        ((2, 96, 320), F32),
        ((2, 2, 2, 320, 640), BF16),
        ((2, 2, 2, 80, 640), BF16),
        ((2, 2, 2, 2, 80, 640), BF16),
        ((2, 2, 2, 80, 640), F32),
        ((2, 2, 80, 640), BF16),
        ((2, 2, 80, 640), BF16),
        ((2, 2, 80, 640), BF16),
        ((16, 128), F32),
        ((8, 16, 128), F32),
        ((4, 16, 128), F32),
        ((16, 128), F32),
    ]
    out = pl.pallas_call(
        lambda *refs: kernel(scale, *refs),
        name="mlp_block",
        out_shape=[
            pltpu.VMEM((192, 320), BF16),
            pltpu.VMEM((192, 320), BF16),
            pltpu.VMEM((2, 320, 1280), BF16),
            pltpu.VMEM((320, 2560), BF16),
            pltpu.VMEM((1280,), BF16),
            pltpu.VMEM((320,), BF16),
        ],
        in_specs=[hbm] * 6,
        out_specs=[vmem] * 6,
        scratch_shapes=[pltpu.VMEM(*s) for s in scratch] + [pltpu.SemaphoreType.DMA((N_SEMS,))],
        compiler_params=pltpu.CompilerParams(
            collective_id=0, has_side_effects=True, vmem_limit_bytes=44 << 20
        ),
        cost_estimate=pl.CostEstimate(
            flops=6 * 2 * 768 * 1280 * 640, bytes_accessed=12 << 20, transcendentals=384 * 640
        ),
    )(
        *[
            pltpu.with_memory_space_constraint(a, pltpu.HBM)
            for a in (
                tokens, up_weight.reshape(2, 320, 1280), up_bias, down_weight.T, down_bias, out_grad
            )
        ]
    )
    layer_out, grad_in, grad_up, grad_down, bu, bd = pl.pallas_call(
        write_back,
        name="write_back",
        out_shape=[jax.ShapeDtypeStruct(a.shape, a.dtype) for a in out],
        in_specs=[vmem] * 6,
        out_specs=[hbm] * 6,
        scratch_shapes=[pltpu.SemaphoreType.DMA((6,))],
        compiler_params=pltpu.CompilerParams(vmem_limit_bytes=1 << 20),
        cost_estimate=pl.CostEstimate(flops=0, bytes_accessed=8 << 20, transcendentals=0),
    )(*[pltpu.with_memory_space_constraint(a, pltpu.VMEM) for a in out])
    return (layer_out, grad_in, grad_up.reshape(640, 1280), bu, grad_down.T, bd)


def solution(mesh):
    return jax.shard_map(
        per_device,
        mesh=mesh,
        in_specs=(
            P(("col", "depth"), "row"),
            P("col", "row"),
            P("row"),
            P("col", "row"),
            P("row"),
            P(("col", "depth"), "row"),
        ),
        out_specs=(
            P(("col", "depth"), "row"),
            P(("col", "depth"), "row"),
            P("col", "row"),
            P("row"),
            P("col", "row"),
            P("row"),
        ),
        check_vma=False,
    )
```

```python
import math

import jax
import jax.numpy as jnp
from jax import lax
from jax.experimental import pallas as pl
from jax.experimental.pallas import tpu as pltpu
from jax.sharding import PartitionSpec as P

GELU_C = math.sqrt(2.0 / math.pi)
MESH = pl.DeviceIdType.MESH
F32 = jnp.float32
BF16 = jnp.bfloat16
N_SEMS = 320


def gelu_parts(v):
    t = jnp.tanh(GELU_C * (v + 0.044715 * v * v * v))
    value = 0.5 * v * (1.0 + t)
    slope = 0.5 * (1.0 + t) + 0.5 * v * (1.0 - t * t) * GELU_C * (1.0 + 3.0 * 0.044715 * v * v)
    return value, slope


def nn(a, b):
    return lax.dot_general(a, b, (((1,), (0,)), ((), ())), preferred_element_type=F32)


def nt(a, b):
    return lax.dot_general(a, b, (((1,), (1,)), ((), ())), preferred_element_type=F32)


def rows(start, size, tile=16):
    return pl.ds(pl.multiple_of(start, tile), size)


def kernel(
    scale,
    tok, wu_in, bu_in, wd_in, bd_in, grad,
    o_out, gi_out, gu_out, gd_out, bu_out, bd_out,
    xo, xr, bu, bd, piece, wq, bb, bbr,
    full, wts, full_t,
    hps, hpr, hpo, slope, act, dhid,
    part, ra, rb, xsum, zr, osend, orecv,
    gpart, ga, gb, gsum, gs, gz, gfin,
    bt, br, yb, pb,
    sems,
):
    row, y, dep = lax.axis_index("row"), lax.axis_index("col"), lax.axis_index("depth")
    h, k = row // 2, lax.rem(row, 2)
    zl, x = dep // 4, lax.rem(dep, 4)
    hh = h // 2
    hi = lax.rem(h, 2)

    def at(h_, k_, y_, plane):
        return (h_ * 2 + k_, y_, plane * 4 + x)

    def is_me(h_, k_, y_, plane):
        return (h_ == h) & (k_ == k) & (y_ == y) & (plane == zl)

    def z_at(a):
        return (lax.rem(h + a, 4) * 2 + k, y, dep)

    def dep_at(a, b):
        return (row, y, lax.rem(zl + b, 2) * 4 + lax.rem(x + a, 4))

    def y_at(a):
        return (row, lax.rem(y + a, 4), dep)

    partner = (h * 2 + 1 - k, y, dep)
    zpeer = dep_at(0, 1)

    local = [
        pltpu.make_async_copy(src, dst, sems.at[n])
        for n, (src, dst) in enumerate(
            (
                (bu_in, bu),
                (tok.at[rows(k * 96, 96)], xo.at[0]),
                (grad.at[rows(k * 96, 96)], xo.at[1]),
                (bd_in, bd),
            )
        )
    ]
    for copy in local:
        copy.start()

    bar = pltpu.get_barrier_semaphore()
    fixed = [partner, z_at(1), z_at(3)] + [y_at(a) for a in (1, 2, 3)]
    fixed += [dep_at(a, b) for a in range(4) for b in range(2) if (a, b) != (0, 0)]
    for target in fixed:
        pl.semaphore_signal(bar, inc=1, device_id=target, device_id_type=MESH)
    count = len(fixed)

    def greet(*place):
        other = jnp.logical_not(is_me(*place))

        @pl.when(other)
        def _():
            pl.semaphore_signal(bar, inc=1, device_id=at(*place), device_id_type=MESH)

        return other.astype(jnp.int32)

    for a in range(4):
        count = count + greet(a, hh, y, zl)
        count = count + greet(y, hh, a, k)
    for a in range(2):
        for b in range(2):
            count = count + greet(2 * k + a, b, y, zl)
            count = count + greet(2 * k + a, zl, h, b)
            count = count + greet(h, y // 2, 2 * k + a, b)
    pl.semaphore_wait(bar, count)

    used = [len(local)]
    sent = []

    def new(n=1):
        first = used[0]
        used[0] += n
        return first

    def send(src, dst, rsem, target):
        copy = pltpu.make_async_remote_copy(
            src_ref=src, dst_ref=dst, send_sem=sems.at[new()], recv_sem=sems.at[rsem],
            device_id=target, device_id_type=MESH,
        )
        copy.start()
        sent.append((copy, None))

    def send_if(only, src, dst, rsem, *place):
        mine = is_me(*place)
        away = jnp.logical_not(mine) & only
        copy = pltpu.make_async_remote_copy(
            src_ref=src, dst_ref=dst, send_sem=sems.at[new()], recv_sem=sems.at[rsem],
            device_id=at(*place), device_id_type=MESH,
        )

        @pl.when(away)
        def _():
            copy.start()

        @pl.when(mine & only)
        def _():
            pltpu.make_async_copy(src, dst, sems.at[rsem]).start()

        sent.append((copy, away))

    def got(dst, rsem):
        pltpu.make_async_copy(dst, dst, sems.at[rsem]).wait()

    def got_if(only, dst, rsem):
        @pl.when(only)
        def _():
            got(dst, rsem)

    def token_view(buf):
        return lambda i, q: buf.at[i, rows(lax.rem(q, 4) * 192, 192)]

    def half_view(buf, i):
        return lambda kk, q: buf.at[i, rows(lax.rem(q, 4) * 192 + kk * 96, 96)]

    def chunk_view(buf):
        return lambda i, q: buf.at[i, :, rows(lax.rem(q, 4) * 80, 80)]

    def chunk_half_view(buf, i):
        return lambda kk, q: buf.at[i, kk, rows(lax.rem(q, 4) * 80, 80)]

    def ring(axis):
        if axis == "y":
            return y, y_at(1), y_at(3)
        return x, dep_at(1, 0), dep_at(3, 0)

    class Gather:
        def __init__(self, view, axis):
            self.p, self.right, self.left = ring(axis)
            self.view = view
            self.s_right, self.s_left, self.s_fwd = new(2), new(2), new(2)

        def first(self, i):
            mine = self.view(i, self.p)
            pair = [(self.s_right + i, self.right), (self.s_left + i, self.left)]
            for sem, target in pair if i == 0 else pair[::-1]:
                send(mine, mine, sem, target)

        def forward(self, i):
            if i == 0:
                block = self.view(0, self.p + 3)
                got(block, self.s_right)
                send(block, block, self.s_fwd, self.right)
            else:
                block = self.view(1, self.p + 1)
                got(block, self.s_left + 1)
                send(block, block, self.s_fwd + 1, self.left)

        def finish(self):
            got(self.view(1, self.p + 3), self.s_right + 1)
            got(self.view(0, self.p + 1), self.s_left)
            got(self.view(0, self.p + 2), self.s_fwd)
            got(self.view(1, self.p + 2), self.s_fwd + 1)

    class Reduce:
        def __init__(self, view, first, second, axis):
            self.p, self.right, self.left = ring(axis)
            self.view = view
            self.first, self.second = first, second
            self.s1, self.s2 = new(2), new(4)

        def far(self):
            send(self.view(0, self.p + 2), self.first.at[0], self.s1, self.right)
            send(self.view(1, self.p + 2), self.first.at[1], self.s1 + 1, self.left)

        def near(self):
            send(self.view(1, self.p + 1), self.second.at[0, 1], self.s2 + 1, self.right)
            send(self.view(0, self.p + 3), self.second.at[1, 0], self.s2 + 2, self.left)

        def middle(self):
            for i, q, target in ((0, self.p + 1, self.right), (1, self.p + 3, self.left)):
                got(self.first.at[i], self.s1 + i)
                block = self.view(i, q)
                block[...] = (block[...].astype(F32) + self.first[i].astype(F32)).astype(BF16)
                send(block, self.second.at[i, i], self.s2 + 3 * i, target)

        def total(self, i):
            got(self.second.at[0, i], self.s2 + i)
            got(self.second.at[1, i], self.s2 + 2 + i)
            return (
                self.view(i, self.p)[...].astype(F32)
                + self.second[0, i].astype(F32)
                + self.second[1, i].astype(F32)
            )

    def pair_lanes(own, other):
        first = jnp.where(k == 0, own, other).astype(F32)
        second = jnp.where(k == 0, other, own).astype(F32)
        return jnp.concatenate([first, second], axis=1).astype(BF16)

    def split_lanes(both):
        low, high = both[:, :320], both[:, 320:]
        return jnp.where(k == 0, low, high), jnp.where(k == 0, high, low)

    s_x = new(2)
    for n, src in enumerate((tok, grad)):
        send(src.at[rows((1 - k) * 96, 96)], xr.at[n], s_x + n, partner)
    quarter = rows(x * 80, 80)
    always = k >= 0
    near = jnp.where(hh == k, hi, 1 - hi)
    order = [near, 1 - near]

    def lanes(n):
        return pl.ds(pl.multiple_of(n * 640, 128), 640)

    s_w = [new(2), new(4)]
    for j in range(2):
        send_if(
            always,
            wu_in.at[:, quarter, pl.ds(j * 640, 640)],
            wts.at[0, lax.rem(y, 2), :, quarter],
            s_w[0] + lax.rem(y, 2), h, y // 2, 2 * k + j, zl,
        )
    s_wq = new(4)
    for a in range(4):
        y_to = lax.rem(y + a, 4)
        send_if(always, wd_in.at[quarter, lanes(y_to)], wq.at[y], s_wq + a, h, k, y_to, zl)
    for copy in local:
        copy.wait()
    bb[...] = jnp.broadcast_to(bu[...].reshape(1, 1280), bb.shape)
    bd_row = bd[...].reshape(1, 320)
    s_bb = new(1)
    send(bb, bbr, s_bb, partner)

    s_piece = [new(4), new(4)]

    def passes(i, kk):
        return h == lax.rem(2 * k + i + (1, 3)[kk], 4)

    def part_of(n, i, kk):
        return full.at[n, i, rows(y * 192 + kk * 96, 96)]

    def send_piece(n):
        got(xr.at[n], s_x + n)
        piece[n] = pair_lanes(xo[n], xr[n])
        dst = part_of(n, hi, k)
        sem = s_piece[n] + hi * 2 + k
        for a in (1, 3):
            send_if(always, piece.at[n], dst, sem, lax.rem(h + a, 4), hh, y, zl)
        send_if(always, piece.at[n], dst, sem, h, hh, y, zl)

    def pass_piece(n):
        for i in range(2):
            for kk, a in ((0, 1), (1, 3)):
                only = passes(i, kk)
                sem = s_piece[n] + i * 2 + kk
                block = part_of(n, i, kk)
                got_if(only, block, sem)
                send_if(only, block, block, sem, lax.rem(h + a, 4), k, y, zl)

    def got_piece(n, i, kk):
        got_if(jnp.logical_not(passes(i, kk)), part_of(n, i, kk), s_piece[n] + i * 2 + kk)

    wag = [Gather(chunk_view(wts.at[n]), "x") for n in range(2)]
    tag = [[Gather(half_view(full.at[n], i), "y") for i in order] for n in range(2)]

    def over_y(n, i, kk):
        got_piece(n, order[i], kk)
        tag[n][i].first(kk)

    send_piece(0)
    for i in range(2):
        got(wts.at[0, i, :, quarter], s_w[0] + i)
        wag[0].first(i)
    pass_piece(0)
    for kk in range(2):
        over_y(0, 0, kk)
    for a in range(4):
        origin = lax.rem(y + 4 - a, 4)
        got(wq.at[origin], s_wq + a)
        send_if(
            always, wq.at[origin], wts.at[1, hi, k, quarter], s_w[1] + hi * 2 + k, origin, hh, y, zl
        )
    for kk in range(2):
        over_y(0, 1, kk)
    send_piece(1)
    for i in range(2):
        wag[0].forward(i)
    for i in range(2):
        for kk in range(2):
            tag[0][i].forward(kk)
    for i in range(2):
        for kk in range(2):
            got(wts.at[1, i, kk, quarter], s_w[1] + i * 2 + kk)
        wag[1].first(i)
    pass_piece(1)
    over_y(1, 0, 0)
    over_y(1, 0, 1)
    over_y(1, 1, 0)

    half = 384
    own_rows = rows(k * half, half)
    other_rows = rows((1 - k) * half, half)

    def weight(n, i):
        return wts[n, i].reshape(640, 640)

    def hidden(n, block):
        return nn(full[n, 0, block], weight(n, 0)) + nn(full[n, 1, block], weight(n, 1))

    def transpose(n, i):
        full_t[n, i] = full[n, i].T.reshape(2, 320, 768)

    s_hp, s_act = [new(1), new(1)], [new(1), new(1)]
    tag[0][0].finish()
    tag[0][1].finish()
    wag[0].finish()
    hps[0] = hidden(0, other_rows)
    send(hps.at[0], hpr.at[0], s_hp[0], partner)
    hpo[...] = hidden(0, own_rows)
    for kk in range(2):
        tag[1][0].forward(kk)
    over_y(1, 1, 1)
    for i in range(2):
        wag[1].forward(i)
    got(bbr, s_bb)
    low = jnp.where(k == y // 2, bb[0:1], bbr[0:1])
    bias = jnp.where(lax.rem(y, 2) == 0, low[:, :640], low[:, 640:])
    got(hpr.at[0], s_hp[0])
    value, slope_now = gelu_parts(hpo[...] + hpr[0] + bias)
    slope[...] = slope_now
    act[own_rows] = value.astype(BF16)
    send(act.at[own_rows], act.at[own_rows], s_act[0], partner)
    for i in range(2):
        transpose(0, i)
    got(act.at[other_rows], s_act[0])

    ored = [Reduce(token_view(part.at[n]), ra.at[n], rb.at[n], "y") for n in range(2)]
    gred = [
        [Reduce(chunk_half_view(gpart.at[n], i), ga.at[n, j], gb.at[n, j], "x") for j, i in enumerate(order)]
        for n in range(2)
    ]

    def out_block(n, q):
        block = rows(lax.rem(q, 4) * 192, 192)
        left = act if n == 0 else dhid
        for i in range(2):
            part[n, i, block] = nt(left[block], weight(1 - n, i)).astype(BF16)

    def grad_block(n, j, q):
        i = order[j]
        block = rows(lax.rem(q, 4) * 80, 80)
        right = dhid if n == 0 else act
        left = full_t[n, i, :, block].reshape(160, 768)
        gpart[n, i, :, block] = (nn(left, right[...]) * scale).astype(BF16).reshape(2, 80, 640)

    def grad_start(n, i):
        grad_block(n, i, x + 2)
        gred[n][i].far()
        grad_block(n, i, x + 1)
        grad_block(n, i, x + 3)
        gred[n][i].near()

    def grad_middle(n, i):
        grad_block(n, i, x)
        gred[n][i].middle()

    s_oz = [new(4), new(4)]

    def out_z(n):
        for i in range(2):
            xsum[n, i] = ored[n].total(i).astype(BF16)
            for kk in range(2):
                send_if(
                    always, xsum.at[n, i, pl.ds(kk * 96, 96)], zr.at[n, h], s_oz[n] + h,
                    2 * k + i, kk, y, zl,
                )

    s_gz, s_gr = [new(2), new(2)], [new(4), new(4)]

    def grad_zl(n, i):
        for kk in range(2):
            gsum[n, i, kk] = gred[n][i].total(kk)
        gs[n, i] = gsum[n, i, 1 - zl].astype(BF16)
        send(gs.at[n, i], gz.at[n, i], s_gz[n] + i, zpeer)

    def grad_home(n, i):
        got(gz.at[n, i], s_gz[n] + i)
        gfin[n, i] = (gsum[n, i, zl] + gz[n, i].astype(F32)).astype(BF16)
        to = 2 * k + order[i]
        for p in range(2):
            plane = lax.rem(zl + 1 - p, 2)
            if n == 0:
                send_if(
                    always, gfin.at[0, i], gu_out.at[zl, quarter, lanes(lax.rem(y, 2))],
                    s_gr[0] + 2 * (1 - p) + lax.rem(y, 2), h, y // 2, to, plane,
                )
            else:
                send_if(
                    always, gfin.at[1, i], gd_out.at[quarter, lanes(y)],
                    s_gr[1] + y, to, zl, h, plane,
                )

    back = [
        Gather(lambda i, q: gu_out.at[:, rows(lax.rem(q, 4) * 80, 80), pl.ds(i * 640, 640)], "x"),
        Gather(lambda i, q: gd_out.at[rows(lax.rem(q, 4) * 80, 80), pl.ds(i * 1280, 1280)], "x"),
    ]

    def back_first(n):
        for i in range(2):
            if n == 0:
                got(gu_out.at[zl, quarter, pl.ds(i * 640, 640)], s_gr[0] + i)
                got(gu_out.at[1 - zl, quarter, pl.ds(i * 640, 640)], s_gr[0] + 2 + i)
            else:
                for j in range(2):
                    got(gd_out.at[quarter, pl.ds((2 * i + j) * 640, 640)], s_gr[1] + 2 * i + j)
            back[n].first(i)

    s_of = [new(1), new(1)]

    def out_last(n):
        total = jnp.zeros((96, 640), F32)
        for a in range(4):
            got(zr.at[n, a], s_oz[n] + a)
            total = total + zr[n, a].astype(F32)
        mine, theirs = split_lanes(total)
        osend[n] = theirs
        send(osend.at[n], orecv.at[n], s_of[n], partner)
        if n == 0:
            o_out[rows(k * 96, 96)] = (mine + bd_row).astype(BF16)
        else:
            gi_out[rows(k * 96, 96)] = mine.astype(BF16)

    tag[1][0].finish()
    transpose(1, order[0])
    grad_start(1, 0)
    for kk in range(2):
        tag[1][1].forward(kk)
    wag[1].finish()
    out_block(0, y + 2)
    ored[0].far()
    grad_middle(1, 0)
    out_block(0, y + 1)
    out_block(0, y + 3)
    ored[0].near()
    tag[1][1].finish()
    hps[1] = hidden(1, other_rows)
    send(hps.at[1], hpr.at[1], s_hp[1], partner)
    transpose(1, order[1])
    grad_start(1, 1)
    d_own = hidden(1, own_rows)
    got(hpr.at[1], s_hp[1])
    dhid[own_rows] = ((d_own + hpr[1]) * slope[...]).astype(BF16)
    send(dhid.at[own_rows], dhid.at[own_rows], s_act[1], partner)
    ored[0].middle()
    grad_zl(1, 0)
    grad_middle(1, 1)
    got(dhid.at[other_rows], s_act[1])
    grad_start(0, 0)
    out_block(1, y + 2)
    ored[1].far()
    grad_home(1, 0)
    grad_start(0, 1)
    grad_zl(1, 1)
    out_block(1, y + 1)
    out_block(1, y + 3)
    ored[1].near()
    grad_middle(0, 0)
    out_block(0, y)
    grad_home(1, 1)
    grad_middle(0, 1)
    ones = jnp.ones((16, 768), BF16)
    terms = [nn(ones, dhid[...]), nn(ones, full[1, 0]), nn(ones, full[1, 1])]
    bt[...] = jnp.zeros_like(bt)
    for n in range(15):
        term = terms[n // 5][0:1, (n % 5) * 128 : (n % 5 + 1) * 128] * scale
        bt[n : n + 1] = term.astype(BF16).astype(F32)
    br[dep] = bt[...]
    s_bt = new(8)
    for a in range(4):
        for b in range(2):
            if (a, b) != (0, 0):
                send(bt, br.at[dep], s_bt + a * 2 + b, dep_at(a, b))
    grad_zl(0, 0)
    ored[1].middle()
    grad_zl(0, 1)
    grad_home(0, 0)
    back_first(1)
    grad_home(0, 1)
    out_z(0)
    out_block(1, y)
    out_z(1)
    for i in range(2):
        back[1].forward(i)

    back_first(0)
    for a in range(4):
        for b in range(2):
            if (a, b) != (0, 0):
                from_dep = lax.rem(zl + b, 2) * 4 + lax.rem(x + 4 - a, 4)
                got(br.at[from_dep], s_bt + a * 2 + b)
    total = br[0]
    for n in range(1, 8):
        total = total + br[n]
    yb[y] = total
    s_yb = new(4)
    for a in range(1, 4):
        send(yb.at[y], yb.at[y], s_yb + a, y_at(a))
    s_pb = new(1)
    send(yb.at[y], pb, s_pb, partner)

    out_last(0)
    for i in range(2):
        back[0].forward(i)
    out_last(1)
    got(orecv.at[0], s_of[0])
    o_out[rows((1 - k) * 96, 96)] = (orecv[0] + bd_row).astype(BF16)
    for a in range(1, 4):
        got(yb.at[lax.rem(y + 4 - a, 4)], s_yb + a)
    got(pb, s_pb)
    wide = [yb[2 * k + j][n : n + 1] for j in range(2) for n in range(5)]
    bu_out[...] = jnp.concatenate(wide, axis=1).astype(BF16).reshape(1280)
    from_tile = jnp.where(k == hh, yb[y], pb[...])
    wide = jnp.concatenate([from_tile[n : n + 1] for n in range(5, 15)], axis=1)
    wide = jnp.where(hi == 0, wide[:, :640], wide[:, 640:])
    bd_out[...] = jnp.where(k == 0, wide[:, :320], wide[:, 320:]).astype(BF16).reshape(320)
    got(orecv.at[1], s_of[1])
    gi_out[rows((1 - k) * 96, 96)] = orecv[1].astype(BF16)
    back[1].finish()
    back[0].finish()

    for copy, when in sent:
        if when is None:
            copy.wait_send()
        else:

            @pl.when(when)
            def _(copy=copy):
                copy.wait_send()

    assert used[0] <= N_SEMS, used[0]


def write_back(*refs):
    sems = refs[-1]
    copies = [
        pltpu.make_async_copy(refs[n], refs[6 + n], sems.at[n]) for n in range(6)
    ]
    for copy in copies:
        copy.start()
    for copy in copies:
        copy.wait()


def per_device(tokens, up_weight, up_bias, down_weight, down_bias, out_grad):
    token_rows = tokens.shape[0]
    scale = 1.0 / math.sqrt(token_rows * lax.axis_size("col") * lax.axis_size("depth"))
    vmem = pl.BlockSpec(memory_space=pltpu.VMEM)
    hbm = pl.BlockSpec(memory_space=pl.ANY)
    scratch = [
        ((2, 96, 320), BF16),
        ((2, 96, 320), BF16),
        ((1280,), F32),
        ((320,), F32),
        ((2, 96, 640), BF16),
        ((4, 80, 640), BF16),
        ((8, 1280), F32),
        ((8, 1280), F32),
        ((2, 2, 768, 640), BF16),
        ((2, 2, 2, 320, 640), BF16),
        ((2, 2, 2, 320, 768), BF16),
        ((2, 384, 640), F32),
        ((2, 384, 640), F32),
        ((384, 640), F32),
        ((384, 640), F32),
        ((768, 640), BF16),
        ((768, 640), BF16),
        ((2, 2, 768, 640), BF16),
        ((2, 2, 192, 640), BF16),
        ((2, 2, 2, 192, 640), BF16),
        ((2, 2, 192, 640), BF16),
        ((2, 4, 96, 640), BF16),
        ((2, 96, 320), F32),
        ((2, 96, 320), F32),
        ((2, 2, 2, 320, 640), BF16),
        ((2, 2, 2, 80, 640), BF16),
        ((2, 2, 2, 2, 80, 640), BF16),
        ((2, 2, 2, 80, 640), F32),
        ((2, 2, 80, 640), BF16),
        ((2, 2, 80, 640), BF16),
        ((2, 2, 80, 640), BF16),
        ((16, 128), F32),
        ((8, 16, 128), F32),
        ((4, 16, 128), F32),
        ((16, 128), F32),
    ]
    out = pl.pallas_call(
        lambda *refs: kernel(scale, *refs),
        name="mlp_block",
        out_shape=[
            pltpu.VMEM((192, 320), BF16),
            pltpu.VMEM((192, 320), BF16),
            pltpu.VMEM((2, 320, 1280), BF16),
            pltpu.VMEM((320, 2560), BF16),
            pltpu.VMEM((1280,), BF16),
            pltpu.VMEM((320,), BF16),
        ],
        in_specs=[hbm] * 6,
        out_specs=[vmem] * 6,
        scratch_shapes=[pltpu.VMEM(*s) for s in scratch] + [pltpu.SemaphoreType.DMA((N_SEMS,))],
        compiler_params=pltpu.CompilerParams(
            collective_id=0, has_side_effects=True, vmem_limit_bytes=44 << 20
        ),
        cost_estimate=pl.CostEstimate(
            flops=6 * 2 * 768 * 1280 * 640, bytes_accessed=12 << 20, transcendentals=384 * 640
        ),
    )(
        *[
            pltpu.with_memory_space_constraint(a, pltpu.HBM)
            for a in (
                tokens, up_weight.reshape(2, 320, 1280), up_bias, down_weight.T, down_bias, out_grad
            )
        ]
    )
    layer_out, grad_in, grad_up, grad_down, bu, bd = pl.pallas_call(
        write_back,
        name="write_back",
        out_shape=[jax.ShapeDtypeStruct(a.shape, a.dtype) for a in out],
        in_specs=[vmem] * 6,
        out_specs=[hbm] * 6,
        scratch_shapes=[pltpu.SemaphoreType.DMA((6,))],
        compiler_params=pltpu.CompilerParams(vmem_limit_bytes=1 << 20),
        cost_estimate=pl.CostEstimate(flops=0, bytes_accessed=8 << 20, transcendentals=0),
    )(*[pltpu.with_memory_space_constraint(a, pltpu.VMEM) for a in out])
    return (layer_out, grad_in, grad_up.reshape(640, 1280), bu, grad_down.T, bd)


def solution(mesh):
    return jax.shard_map(
        per_device,
        mesh=mesh,
        in_specs=(
            P(("col", "depth"), "row"),
            P("col", "row"),
            P("row"),
            P("col", "row"),
            P("row"),
            P(("col", "depth"), "row"),
        ),
        out_specs=(
            P(("col", "depth"), "row"),
            P(("col", "depth"), "row"),
            P("col", "row"),
            P("row"),
            P("col", "row"),
            P("row"),
        ),
        check_vma=False,
    )
```
